128 devices in a mesh: ha: 4 (over z), wa: 4 (over y), img: 8 (over x, core).
Axes of the slice: x: 4, y: 4, z: 4, core: 2. Of those that a mesh axis runs over, the one named last changes fastest.
Arguments:
- images: bfloat16 [512, 40, 40, 192], P('img', 'ha', 'wa'), may hold values from -6 to 6
- classes: int32 [512], replicated, may hold values from 0 to 2, as said below
- image_counts: int32 [8], replicated, may hold values from 32 to 64, as said below
- entry_kernel: bfloat16 [192, 512], replicated, may hold values from -0.4375 to 0.4375
- entry_gain: float32 [512], replicated, may hold values from 0.5 to 1.5
- entry_shift: float32 [512], replicated, may hold values from -1.8 to 1.8
- group_kernel: bfloat16 [3, 3, 64, 512], replicated, may hold values from -0.25 to 0.25
- group_gain: float32 [512], replicated, may hold values from 0.5 to 1.5
- group_shift: float32 [512], replicated, may hold values from -1.8 to 1.8
- squeeze_weight: bfloat16 [512, 48], replicated, may hold values from -0.5 to 0.5
- squeeze_bias: float32 [48], replicated, may hold values from -3 to 3
- excite_weight: bfloat16 [48, 512], replicated, may hold values from -0.875 to 0.875
- excite_bias: float32 [512], replicated, may hold values from -3 to 3
- output_kernel: bfloat16 [512, 512], replicated, may hold values from -0.25 to 0.25
- output_gain: float32 [512], replicated, may hold values from 0.5 to 1.5
- output_shift: float32 [512], replicated, may hold values from -1.8 to 1.8
- shortcut_kernel: bfloat16 [192, 512], replicated, may hold values from -0.4375 to 0.4375
- shortcut_gain: float32 [512], replicated, may hold values from 0.5 to 1.5
- shortcut_shift: float32 [512], replicated, may hold values from -1.8 to 1.8
- second_kernel: bfloat16 [512, 512], replicated, may hold values from -0.25 to 0.25
- second_gain: float32 [512], replicated, may hold values from 0.5 to 1.5
- second_shift: float32 [512], replicated, may hold values from -1.8 to 1.8
- spatial_kernel: bfloat16 [3, 3, 64, 512], replicated, may hold values from -0.25 to 0.25
- spatial_gain: float32 [512], replicated, may hold values from 0.5 to 1.5
- spatial_shift: float32 [512], replicated, may hold values from -1.8 to 1.8
- reduce_weight: bfloat16 [512, 128], replicated, may hold values from -0.5 to 0.5
- reduce_bias: float32 [128], replicated, may hold values from -3 to 3
- expand_weight: bfloat16 [128, 512], replicated, may hold values from -0.5 to 0.5
- expand_bias: float32 [512], replicated, may hold values from -3 to 3
- final_kernel: bfloat16 [512, 512], replicated, may hold values from -0.25 to 0.25
- final_gain: float32 [512], replicated, may hold values from 0.5 to 1.5
- final_shift: float32 [512], replicated, may hold values from -1.8 to 1.8
- cotangent: bfloat16 [512, 20, 20, 512], P('img', 'ha', 'wa'), may hold values from -6 to 6
Outputs:
- activations: bfloat16 [512, 20, 20, 512], P('img', 'ha', 'wa')
- images_grad: bfloat16 [512, 40, 40, 192], P('img', 'ha', 'wa')
- grad_entry_kernel: float32 [192, 512], replicated
- grad_entry_gain: float32 [512], replicated
- grad_entry_shift: float32 [512], replicated
- grad_group_kernel: float32 [3, 3, 64, 512], replicated
- grad_group_gain: float32 [512], replicated
- grad_group_shift: float32 [512], replicated
- grad_squeeze_weight: float32 [512, 48], replicated
- grad_squeeze_bias: float32 [48], replicated
- grad_excite_weight: float32 [48, 512], replicated
- grad_excite_bias: float32 [512], replicated
- grad_output_kernel: float32 [512, 512], replicated
- grad_output_gain: float32 [512], replicated
- grad_output_shift: float32 [512], replicated
- grad_shortcut_kernel: float32 [192, 512], replicated
- grad_shortcut_gain: float32 [512], replicated
- grad_shortcut_shift: float32 [512], replicated
- grad_second_kernel: float32 [512, 512], replicated
- grad_second_gain: float32 [512], replicated
- grad_second_shift: float32 [512], replicated
- grad_spatial_kernel: float32 [3, 3, 64, 512], replicated
- grad_spatial_gain: float32 [512], replicated
- grad_spatial_shift: float32 [512], replicated
- grad_reduce_weight: float32 [512, 128], replicated
- grad_reduce_bias: float32 [128], replicated
- grad_expand_weight: float32 [128, 512], replicated
- grad_expand_bias: float32 [512], replicated
- grad_final_kernel: float32 [512, 512], replicated
- grad_final_gain: float32 [512], replicated
- grad_final_shift: float32 [512], replicated
The draws below stay inside these ranges and needn't reach their ends.
Inputs may be any that keep to these rules, and one draw needn't show every extreme that they name: `classes`: every index of img holds a live image of class 2. `image_counts`: live images fill the first slots of an index; one index holds 64 images and another 64 // 2.
All inputs are finite; a program needn't handle non-finite values.
Results may differ from the reference program's by a relative error of at most 0.028.
Values may be sent and summed in bfloat16 or wider, within the bound.
A program may use at most 384 MiB of HBM per device.

```python
from functools import partial
import jax
import jax.numpy as jnp
from jax import lax

SLOTS = 64
C_IN = 192
C_OUT = 512
GROUP_WIDTH = 64
SE_FIRST = 48
SE_SECOND = 128
GRID = 20
IMAGES = 512
N_IMG = 8


def pick_full(key):
    return jax.random.randint(jax.random.fold_in(key, 7), (), 0, N_IMG)


def draw_image_counts(key, part):
    full_index = pick_full(key)
    key = jax.random.fold_in(key, 1)
    key_one, key_two = jax.random.split(key)
    base_counts = jax.random.randint(key_one, (N_IMG,), SLOTS // 2, SLOTS + 1)
    light_index = (full_index + 1 + jax.random.randint(key_two, (), 0, N_IMG - 1)) % N_IMG
    positions = jnp.arange(N_IMG)
    chosen = jnp.where(positions == light_index, SLOTS // 2, base_counts)
    return jnp.where(positions == full_index, SLOTS, chosen).astype(jnp.int32)


def draw_classes(key, part):
    counts = draw_image_counts(key, part)
    key = jax.random.fold_in(key, 2)
    key_one, key_two = jax.random.split(key)
    base_classes = jax.random.randint(key_one, (IMAGES,), 0, 3)
    slot_pick = jax.random.randint(key_two, (N_IMG,), 0, counts)
    positions = jnp.arange(IMAGES)
    forced = positions % SLOTS == jnp.repeat(slot_pick, SLOTS)
    return jnp.where(forced, 2, base_classes).astype(jnp.int32)


def levels(rng, dims, cuts, low, high):
    def one(position, parts):
        draws = jax.random.uniform(jax.random.fold_in(jax.random.fold_in(rng, 6), position), (parts,), jnp.float32, low / len(cuts), high / len(cuts))
        return jnp.repeat(jnp.exp(draws), dims[position] // parts).reshape((-1,) + (1,) * (len(dims) - position - 1))

    loudness = one(*cuts[0])
    for cut in cuts[1:]:
        loudness = loudness * one(*cut)
    return loudness


def scatter_about(stream_key, shape, scale, reach, cuts=(), kind=jnp.bfloat16):
    values = jax.random.normal(stream_key, shape, jnp.float32) * scale
    if len(cuts) > 0:
        values = levels(stream_key, shape, cuts, -0.22, 0.18) * values
    return jnp.clip(values, min=-reach, max=reach).astype(kind)


def setup_inputs(seed: int = 0) -> dict:
    keys = jax.random.split(jax.random.key(seed), 34)
    images = scatter_about(keys[0], (IMAGES, 2 * GRID, 2 * GRID, C_IN), 1.0, 6.0, ((0, 8), (1, 4), (2, 4)))
    classes = draw_classes(jax.random.fold_in(keys[33], 71), 0)
    image_counts = draw_image_counts(jax.random.fold_in(keys[33], 71), 0)
    entry_kernel = scatter_about(keys[3], (C_IN, C_OUT), C_IN ** -0.5, 0.4375)
    entry_gain = jnp.clip(1.0 + 0.1 * jax.random.normal(keys[4], (C_OUT,), jnp.float32), 0.5, 1.5)
    entry_shift = scatter_about(keys[5], (C_OUT,), 0.3, 1.8, (), jnp.float32)
    group_kernel = scatter_about(keys[6], (3, 3, GROUP_WIDTH, C_OUT), (9 * GROUP_WIDTH) ** -0.5, 0.25)
    group_gain = jnp.clip(1.0 + 0.1 * jax.random.normal(keys[7], (C_OUT,), jnp.float32), 0.5, 1.5)
    group_shift = scatter_about(keys[8], (C_OUT,), 0.3, 1.8, (), jnp.float32)
    squeeze_weight = scatter_about(keys[9], (C_OUT, SE_FIRST), (C_OUT // 4) ** -0.5, 0.5)
    squeeze_bias = scatter_about(keys[10], (SE_FIRST,), 0.5, 3.0, (), jnp.float32)
    excite_weight = scatter_about(keys[11], (SE_FIRST, C_OUT), SE_FIRST ** -0.5, 0.875)
    excite_bias = scatter_about(keys[12], (C_OUT,), 0.5, 3.0, (), jnp.float32)
    output_kernel = scatter_about(keys[13], (C_OUT, C_OUT), C_OUT ** -0.5, 0.25)
    output_gain = jnp.clip(1.0 + 0.1 * jax.random.normal(keys[14], (C_OUT,), jnp.float32), 0.5, 1.5)
    output_shift = scatter_about(keys[15], (C_OUT,), 0.3, 1.8, (), jnp.float32)
    shortcut_kernel = scatter_about(keys[16], (C_IN, C_OUT), C_IN ** -0.5, 0.4375)
    shortcut_gain = jnp.clip(1.0 + 0.1 * jax.random.normal(keys[17], (C_OUT,), jnp.float32), 0.5, 1.5)
    shortcut_shift = scatter_about(keys[18], (C_OUT,), 0.3, 1.8, (), jnp.float32)
    second_kernel = scatter_about(keys[19], (C_OUT, C_OUT), C_OUT ** -0.5, 0.25)
    second_gain = jnp.clip(1.0 + 0.1 * jax.random.normal(keys[20], (C_OUT,), jnp.float32), 0.5, 1.5)
    second_shift = scatter_about(keys[21], (C_OUT,), 0.3, 1.8, (), jnp.float32)
    spatial_kernel = scatter_about(keys[22], (3, 3, GROUP_WIDTH, C_OUT), (9 * GROUP_WIDTH) ** -0.5, 0.25)
    spatial_gain = jnp.clip(1.0 + 0.1 * jax.random.normal(keys[23], (C_OUT,), jnp.float32), 0.5, 1.5)
    spatial_shift = scatter_about(keys[24], (C_OUT,), 0.3, 1.8, (), jnp.float32)
    reduce_weight = scatter_about(keys[25], (C_OUT, SE_SECOND), (C_OUT // 4) ** -0.5, 0.5)
    reduce_bias = scatter_about(keys[26], (SE_SECOND,), 0.5, 3.0, (), jnp.float32)
    expand_weight = scatter_about(keys[27], (SE_SECOND, C_OUT), SE_SECOND ** -0.5, 0.5)
    expand_bias = scatter_about(keys[28], (C_OUT,), 0.5, 3.0, (), jnp.float32)
    final_kernel = scatter_about(keys[29], (C_OUT, C_OUT), C_OUT ** -0.5, 0.25)
    final_gain = jnp.clip(1.0 + 0.1 * jax.random.normal(keys[30], (C_OUT,), jnp.float32), 0.5, 1.5)
    final_shift = scatter_about(keys[31], (C_OUT,), 0.3, 1.8, (), jnp.float32)
    cotangent = scatter_about(keys[32], (IMAGES, GRID, GRID, C_OUT), 1.0, 6.0, ((0, 8), (1, 4), (2, 4)))
    return {"images": images, "classes": classes, "image_counts": image_counts, "entry_kernel": entry_kernel, "entry_gain": entry_gain, "entry_shift": entry_shift, "group_kernel": group_kernel, "group_gain": group_gain, "group_shift": group_shift, "squeeze_weight": squeeze_weight, "squeeze_bias": squeeze_bias, "excite_weight": excite_weight, "excite_bias": excite_bias, "output_kernel": output_kernel, "output_gain": output_gain, "output_shift": output_shift, "shortcut_kernel": shortcut_kernel, "shortcut_gain": shortcut_gain, "shortcut_shift": shortcut_shift, "second_kernel": second_kernel, "second_gain": second_gain, "second_shift": second_shift, "spatial_kernel": spatial_kernel, "spatial_gain": spatial_gain, "spatial_shift": spatial_shift, "reduce_weight": reduce_weight, "reduce_bias": reduce_bias, "expand_weight": expand_weight, "expand_bias": expand_bias, "final_kernel": final_kernel, "final_gain": final_gain, "final_shift": final_shift, "cotangent": cotangent}


EPS = 1e-05
HIGH = lax.Precision.HIGHEST

@jax.custom_vjp
def low(v):
    return lax.optimization_barrier(v.astype(jnp.bfloat16)).astype(jnp.float32)

@jax.custom_vjp
def low_back(v):
    return v

def low_keep(v):
    return (low(v), None)

def low_pass(kept, grad):
    return (grad,)

def back_keep(v):
    return (v, None)

def back_low(kept, grad):
    return (low(grad),)
low.defvjp(low_keep, low_pass)
low_back.defvjp(back_keep, back_low)

def image_masks(classes, image_counts):
    positions = jnp.arange(IMAGES, dtype=jnp.int32)
    occupied = (positions % SLOTS < jnp.repeat(image_counts, SLOTS)).astype(jnp.float32)
    side_out = 10 + 4 * classes
    cells_in = jnp.arange(2 * GRID, dtype=jnp.int32)
    cells_out = jnp.arange(GRID, dtype=jnp.int32)
    inner_in = (cells_in[None, :] < 2 * side_out[:, None]).astype(jnp.float32)
    inner_out = (cells_out[None, :] < side_out[:, None]).astype(jnp.float32)
    mask_in = occupied[:, None, None] * inner_in[:, :, None] * inner_in[:, None, :]
    mask_out = occupied[:, None, None] * inner_out[:, :, None] * inner_out[:, None, :]
    pixels = (side_out * side_out).astype(jnp.float32)
    return (mask_in[..., None], mask_out[..., None], pixels)

def normalize(field, region, cell_count, gain_values, shift_values):
    weighted = field * region
    center = lax.optimization_barrier(jnp.sum(weighted, axis=(0, 1, 2))) / cell_count
    second_moment = lax.optimization_barrier(jnp.sum(weighted * field, axis=(0, 1, 2))) / cell_count
    factor = lax.rsqrt(second_moment - center * center + EPS)
    return (field - center) * factor * gain_values + shift_values

def project(field, matrix):
    return jnp.einsum('nhwc,cd->nhwd', field, matrix, precision=HIGH)

def grouped(field, kernel, stride):
    return lax.conv_general_dilated(field, kernel, (stride, stride), ((1, 1), (1, 1)), dimension_numbers=('NHWC', 'HWIO', 'NHWC'), precision=HIGH)

def excite(gated, pixels, down_weight, down_bias, upward, up_bias):
    pooled = lax.optimization_barrier(jnp.sum(gated, axis=(1, 2))) / pixels[:, None]
    hidden = jax.nn.silu(jnp.dot(pooled, down_weight, precision=HIGH) + down_bias)
    factor = jax.nn.sigmoid(jnp.dot(hidden, upward, precision=HIGH) + up_bias)
    return gated * factor[:, None, None, :]

def split_columns(matrix, pieces):
    return jnp.transpose(matrix.reshape(matrix.shape[0], pieces, -1), (1, 0, 2))

def split_vector(vector, pieces):
    return vector.reshape(pieces, -1)

def split_kernel(kernel, pieces):
    return jnp.transpose(kernel.reshape(3, 3, kernel.shape[2], pieces, -1), (3, 0, 1, 2, 4))

def split_field(field, pieces):
    return jnp.transpose(field.reshape(field.shape[:3] + (pieces, -1)), (3, 0, 1, 2, 4))

def join_field(stacked):
    return jnp.transpose(stacked, (1, 2, 3, 0, 4)).reshape(stacked.shape[1:4] + (-1,))

def forward(context, source, entry_kernel, entry_gain, entry_shift, group_kernel, group_gain, group_shift, squeeze_weight, squeeze_bias, excite_weight, excite_bias, output_kernel, output_gain, output_shift, shortcut_kernel, shortcut_gain, shortcut_shift, second_kernel, second_gain, second_shift, spatial_kernel, spatial_gain, spatial_shift, reduce_weight, reduce_bias, expand_weight, expand_bias, final_kernel, final_gain, final_shift):
    mask_in, mask_out, pixels, cells_in, cells_out = context
    pieces = group_kernel.shape[3] // group_kernel.shape[2]
    start = source * mask_in
    strided = start[:, ::2, ::2, :]

    def first_path(blocks):
        kernel_in, gain_in, shift_in, kernel_mid, gain_mid, shift_mid = blocks
        entry = low_back(project(start, kernel_in))
        active = low(jax.nn.silu(normalize(entry, mask_in, cells_in, gain_in, shift_in)) * mask_in)
        middle = low_back(grouped(active, kernel_mid, 2))
        return jax.nn.silu(normalize(middle, mask_out, cells_out, gain_mid, shift_mid)) * mask_out
    gated = join_field(lax.map(jax.checkpoint(first_path), (split_columns(entry_kernel, pieces), split_vector(entry_gain, pieces), split_vector(entry_shift, pieces), split_kernel(group_kernel, pieces), split_vector(group_gain, pieces), split_vector(group_shift, pieces))))
    excited = low(excite(gated, pixels, squeeze_weight, squeeze_bias, excite_weight, excite_bias))

    def first_tail(blocks):
        kernel_out, gain_out, shift_out, kernel_skip, gain_skip, shift_skip = blocks
        branch = low_back(project(excited, kernel_out))
        bypass = low_back(project(strided, kernel_skip))
        summed = normalize(branch, mask_out, cells_out, gain_out, shift_out) + normalize(bypass, mask_out, cells_out, gain_skip, shift_skip)
        return low(jax.nn.silu(summed) * mask_out)
    middle_out = join_field(lax.map(jax.checkpoint(first_tail), (split_columns(output_kernel, pieces), split_vector(output_gain, pieces), split_vector(output_shift, pieces), split_columns(shortcut_kernel, pieces), split_vector(shortcut_gain, pieces), split_vector(shortcut_shift, pieces))))

    def second_path(blocks):
        kernel_in, gain_in, shift_in, kernel_mid, gain_mid, shift_mid = blocks
        entry = low_back(project(middle_out, kernel_in))
        active = low(jax.nn.silu(normalize(entry, mask_out, cells_out, gain_in, shift_in)) * mask_out)
        middle = low_back(grouped(active, kernel_mid, 1))
        return jax.nn.silu(normalize(middle, mask_out, cells_out, gain_mid, shift_mid)) * mask_out
    gated_two = join_field(lax.map(jax.checkpoint(second_path), (split_columns(second_kernel, pieces), split_vector(second_gain, pieces), split_vector(second_shift, pieces), split_kernel(spatial_kernel, pieces), split_vector(spatial_gain, pieces), split_vector(spatial_shift, pieces))))
    excited_two = low(excite(gated_two, pixels, reduce_weight, reduce_bias, expand_weight, expand_bias))

    def second_tail(blocks):
        kernel_out, gain_out, shift_out, residual = blocks
        branch = low_back(project(excited_two, kernel_out))
        return jax.nn.silu(normalize(branch, mask_out, cells_out, gain_out, shift_out) + residual) * mask_out
    return join_field(lax.map(jax.checkpoint(second_tail), (split_columns(final_kernel, pieces), split_vector(final_gain, pieces), split_vector(final_shift, pieces), split_field(middle_out, pieces))))

def reference(images, classes, image_counts, entry_kernel, entry_gain, entry_shift, group_kernel, group_gain, group_shift, squeeze_weight, squeeze_bias, excite_weight, excite_bias, output_kernel, output_gain, output_shift, shortcut_kernel, shortcut_gain, shortcut_shift, second_kernel, second_gain, second_shift, spatial_kernel, spatial_gain, spatial_shift, reduce_weight, reduce_bias, expand_weight, expand_bias, final_kernel, final_gain, final_shift, cotangent):
    mask_in, mask_out, pixels = image_masks(classes, image_counts)
    context = (mask_in, mask_out, pixels, jnp.sum(mask_in), jnp.sum(mask_out))
    weights = (entry_kernel, entry_gain, entry_shift, group_kernel, group_gain, group_shift, squeeze_weight, squeeze_bias, excite_weight, excite_bias, output_kernel, output_gain, output_shift, shortcut_kernel, shortcut_gain, shortcut_shift, second_kernel, second_gain, second_shift, spatial_kernel, spatial_gain, spatial_shift, reduce_weight, reduce_bias, expand_weight, expand_bias, final_kernel, final_gain, final_shift)
    floats = tuple((weight.astype(jnp.float32) for weight in weights))
    outcome, pullback = jax.vjp(partial(forward, context), images.astype(jnp.float32), *floats)
    grads = pullback(cotangent.astype(jnp.float32))
    return (outcome.astype(jnp.bfloat16), grads[0].astype(jnp.bfloat16), grads[1], grads[2], grads[3], grads[4], grads[5], grads[6], grads[7], grads[8], grads[9], grads[10], grads[11], grads[12], grads[13], grads[14], grads[15], grads[16], grads[17], grads[18], grads[19], grads[20], grads[21], grads[22], grads[23], grads[24], grads[25], grads[26], grads[27], grads[28], grads[29])
```

```python
import functools
import types

import jax
import jax.numpy as jnp
from jax import lax
from jax.experimental import pallas as pl
from jax.experimental.pallas import tpu as pltpu
from jax.sharding import PartitionSpec as P

EPS = 1e-05
F32 = jnp.float32
BF16 = jnp.bfloat16
MESH = pl.DeviceIdType.MESH
FAR = 1 << 20
LANES = 128

(
    ENTRY_G, ENTRY_S, GROUP_G, GROUP_S, OUTPUT_G, OUTPUT_S, SHORT_G, SHORT_S, SECOND_G, SECOND_S,
    SPATIAL_G, SPATIAL_S, FINAL_G, FINAL_S, EXCITE_B, EXPAND_B, SQUEEZE_B, REDUCE_B,
) = range(18)

A_, S_, B_, C_, D_, E_, F_ = range(7)
(SUM_A, SUM_B, SUM_C, SUM_D, SUM_E, SUM_F, BACK_F, BACK_E, BACK_D, BACK_C, BACK_B, BACK_A) = range(12)
VECTORS = (4, 2, 2, 2, 2, 2, 2, 2, 2, 3, 2, 2)

PARITY_TAPS = (4, 3, 5, 1, 7, 0, 2, 6, 8)
PARITY_SPANS = {(0, 0): (0, 1), (0, 1): (1, 3), (1, 0): (3, 5), (1, 1): (5, 9)}


def mm(a, b):
    return lax.dot_general(a, b, (((1,), (0,)), ((), ())), preferred_element_type=F32)


def mt(a, b):
    return lax.dot_general(a, b, (((1,), (1,)), ((), ())), preferred_element_type=F32)


def tm(a, b):
    return lax.dot_general(a, b, (((0,), (0,)), ((), ())), preferred_element_type=F32)


def exact_tm(a, b):
    return lax.dot_general(
        a, b, (((0,), (0,)), ((), ())), precision=lax.Precision.HIGHEST, preferred_element_type=F32
    )


def split_rows(a):
    high = a.astype(BF16)
    return jnp.concatenate([high, (a - high.astype(F32)).astype(BF16)], axis=0)


def fine(product, a, b):
    both = product(split_rows(a), b)
    return both[: a.shape[0]] + both[a.shape[0] :]


def fold(v):
    return jnp.sum(v.reshape(v.shape[0] // 8, 8, v.shape[1]), axis=0)


def sigmoid(v):
    return 0.5 * jnp.tanh(0.5 * v) + 0.5


def silu_half(y):
    return y * jnp.tanh(y) + y


def silu_and_slope(y):
    t = jnp.tanh(y)
    u = y * t
    return y + u, (1.0 + t) * (1.0 + (y - u))


def in_parts(v, count):
    parts = []
    for _ in range(count):
        parts.append(v.astype(BF16))
        v = v - parts[-1].astype(F32)
    return parts


def exact(product, a, b):
    (a_high, a_low), (b_high, b_low) = in_parts(a, 2), in_parts(b, 2)
    return product(a_high, b_high) + (product(a_low, b_high) + product(a_high, b_low))


def spread_lanes(m, width):
    whole, rest = divmod(width, LANES)
    parts = [m] * whole + ([m[:, :rest]] if rest else [])
    return parts[0] if len(parts) == 1 else jnp.concatenate(parts, axis=1)


def grad_rows(channels, inputs, hidden_one, hidden_two, width):
    groups = (
        dict(final=channels, reduce=hidden_two, expand=hidden_two, spatial=9 * width),
        dict(
            second=channels, output=channels, shortcut=inputs, squeeze=hidden_one, excite=hidden_one, biases=16
        ),
        dict(group=9 * width),
        dict(entry=inputs),
    )
    at, rows, jobs = 0, {}, []
    for group in groups:
        first = at
        for name, size in group.items():
            rows[name] = (at, size)
            at += size
        at = first + -(-(at - first) // LANES) * LANES
        jobs.append((first, at - first))
    return rows, jobs, at


def kernel(d, *refs):
    s = types.SimpleNamespace(**dict(zip(d.names, refs, strict=True)))
    n, c, ci, r_out, nch = d.images, d.channels, d.inputs, d.rows, d.channels // LANES
    ca = d.augmented
    half = min(256, c)
    halves = c // half
    width = d.width
    h_in = 2 * r_out
    block = r_out * n
    points = r_out * block
    group = n // d.ha
    plane = d.ha * d.wa
    chips = d.img // 2
    ha, wa, img = lax.axis_index("ha"), lax.axis_index("wa"), lax.axis_index("img")
    core, chip = img % 2, img // 2
    here = ha * d.wa + wa
    row0, col0 = ha * h_in, wa * h_in
    along_z = [ha] + [(ha + i) % d.ha for i in range(1, d.ha)]
    along_y = [wa] + [(wa + i) % d.wa for i in range(1, d.wa)]
    along_img = [img] + [(img + i) % d.img for i in range(1, d.img)]
    along_x = [2 * ((chip + i) % chips) + core for i in range(1, chips)]
    plane_peers = [(z, y) for z in along_z for y in along_y][1:]
    partner = (ha, wa, img + 1 - 2 * core)

    at = types.SimpleNamespace(**{name: first for name, (first, _) in d.grad_rows.items()})


    def beside(dr, dc):
        return (along_z[dr % d.ha], along_y[dc % d.wa], img)

    def place(g, total):
        return jnp.where(jnp.logical_or(g < 0, g >= total), FAR, g)

    def mask_at(gr, gc, lanes, value=1.0):
        far = jnp.maximum(place(gr, d.ha * h_in), place(gc, d.wa * h_in))
        return spread_lanes(jnp.where(s.lim[...] > far, value, 0.0).astype(F32), lanes)

    def masks_out(r, value=1.0):
        return [mask_at(row0 + 2 * r, col0 + 2 * j, half, value) for j in range(r_out)]

    def rows(r):
        return pl.ds(pl.multiple_of(r * block, block), block)

    def spot(r, j):
        return pl.ds(pl.multiple_of(r * block + j * n, n), n)

    def lanes(k):
        return slice(k * half, (k + 1) * half)

    def quarter(q):
        return slice(q * LANES, (q + 1) * LANES)

    def part(v, j):
        return v[j * n : (j + 1) * n]

    def vec(i):
        return s.vec[i : i + 1, :]

    pieces = [(j, k) for k in range(halves) for j in range(r_out)]

    def over(folds, images, body, steps=r_out):
        def step(r, carry):
            held = list(carry)

            def add(i, k, v):
                held[i * halves + k] = held[i * halves + k] + fold(v)

            def add_image(i, k, v):
                held[(folds + i) * halves + k] = held[(folds + i) * halves + k] + v

            body(r, add, add_image)
            return tuple(held)

        start = (jnp.zeros((8, half), F32),) * (folds * halves) + (jnp.zeros((n, half), F32),) * (images * halves)
        out = lax.fori_loop(0, steps, step, start)
        return [jnp.concatenate(out[i * halves : (i + 1) * halves], axis=1) for i in range(folds + images)]

    def over_rows(count, body):
        return over(count, 0, lambda r, add, _: body(r, add))

    def each_row(body, steps=r_out, first=0):
        def step(r, carry):
            body(r)
            return carry

        lax.fori_loop(first, steps, step, 0)


    def vector_rows(k):
        return -(-2 * nch // 8) * 8 * (2 if k in wide else 1)

    wide = [k for k, count in enumerate(VECTORS) if count > 2]

    def places_of(k):
        if k in wide:
            return s.slots_wide.at[wide.index(k)], s.across_wide.at[wide.index(k)]
        return s.slots.at[k], s.across.at[k]

    def sum_start(k, parts):
        slots, _ = places_of(k)
        lines = vector_rows(k)
        if lines > len(parts) * nch:
            slots[here] = jnp.zeros((lines, LANES), F32)
        for j, value in enumerate(parts):
            total = jnp.sum(value, axis=0, keepdims=True)
            for i in range(nch):
                line = j * nch + i
                slots[here, line : line + 1, :] = total[:, i * LANES : (i + 1) * LANES]
        mine = slots.at[here]
        for z, y in plane_peers:
            pltpu.make_async_remote_copy(
                src_ref=mine, dst_ref=mine, send_sem=s.sum_sems.at[k, 0], recv_sem=s.sum_sems.at[k, 1],
                device_id=(z, y, img), device_id_type=MESH,
            ).start()

    def sum_wait(k, sem):
        got = places_of(k)[0].at[pl.ds(0, plane - 1)]
        pltpu.make_async_copy(got, got, s.sum_sems.at[k, sem]).wait()

    def sum_wait_across(k, sem):
        got = places_of(k)[1].at[pl.ds(0, d.img - 1)]
        pltpu.make_async_copy(got, got, s.sum_sems.at[k, sem]).wait()

    def sum_finish(k):
        slots, across = places_of(k)
        lines = vector_rows(k)
        sum_wait(k, 1)
        total = slots[0]
        for i in range(1, plane):
            total = total + slots[i]
        across[img] = total
        mine = across.at[img]
        for x in along_img[1:]:
            pltpu.make_async_remote_copy(
                src_ref=mine, dst_ref=mine, send_sem=s.sum_sems.at[k, 2], recv_sem=s.sum_sems.at[k, 3],
                device_id=(ha, wa, x), device_id_type=MESH,
            ).start()
        sum_wait_across(k, 3)
        total = across[0]
        for i in range(1, d.img):
            total = total + across[i]
        s.reduced[0:lines, :] = total
        return [
            jnp.concatenate([s.reduced[j * nch + i : j * nch + i + 1, :] for i in range(nch)], axis=1)
            for j in range(VECTORS[k])
        ]

    def keep(m, i, k=None):
        return s.keep[8 * m + i : 8 * m + i + 1, slice(None) if k is None else lanes(k)]

    def set_norm(m, total, square, inverse, gain, shift):
        center = total * inverse
        factor = lax.rsqrt(square * inverse - center * center + EPS)
        scale = factor * vec(gain)
        offset = vec(shift) - center * scale
        for i, value in enumerate((center, factor, 0.5 * scale, 0.5 * offset, scale)):
            s.keep[8 * m + i : 8 * m + i + 1, :] = value

    def set_back(m, shift_sum, weighted, inverse, out, raised=0.0):
        center, factor, scale = keep(m, 0), keep(m, 1), keep(m, 4)
        gain_sum = (weighted - (center + raised) * shift_sum) * factor
        slope = -(scale * factor * gain_sum * inverse)
        offset = -(scale * shift_sum * inverse) - slope * center
        for i, value in enumerate((scale, slope, offset)):
            s.keep[8 * m + 5 + i : 8 * m + 6 + i, :] = value
        s.vectors[out : out + 1, :] = gain_sum
        s.vectors[out + 1 : out + 2, :] = shift_sum

    def back(m, upstream, field, mask, k):
        return (upstream * keep(m, 5, k) + (field * keep(m, 6, k) + keep(m, 7, k)) * mask).astype(BF16)


    def tiles_start(e, terms):
        s.tile_slots[e, here, :, 0 : terms.shape[1]] = terms.astype(BF16)
        mine = s.tile_slots.at[e, here]
        for z, y in plane_peers:
            pltpu.make_async_remote_copy(
                src_ref=mine, dst_ref=mine, send_sem=s.tile_sems.at[e, 0], recv_sem=s.tile_sems.at[e, 1],
                device_id=(z, y, img), device_id_type=MESH,
            ).start()

    def tiles_wait(e, sem):
        got = s.tile_slots.at[e, pl.ds(0, plane - 1)]
        pltpu.make_async_copy(got, got, s.tile_sems.at[e, sem]).wait()

    def tiles_finish(e, units):
        tiles_wait(e, 1)
        total = s.tile_slots[e, 0].astype(F32)
        for i in range(1, plane):
            total = total + s.tile_slots[e, i].astype(F32)
        return total[:, 0:units]

    def gates_load(parts):
        for i, value in enumerate(parts):
            s.gate_src[:, i] = value.astype(BF16).reshape(d.ha, group, c)

    def gates_start(which):
        s.gate_slots[here] = s.gate_src[ha]
        for z, y in plane_peers:
            pltpu.make_async_remote_copy(
                src_ref=s.gate_src.at[z], dst_ref=s.gate_slots.at[here], send_sem=s.gate_sems.at[which, 0],
                recv_sem=s.gate_sems.at[which, 1], device_id=(z, y, img), device_id_type=MESH,
            ).start()

    def gates_finish(which):
        got = s.gate_slots.at[pl.ds(0, plane - 1)]
        pltpu.make_async_copy(got, got, s.gate_sems.at[which, 1]).wait()
        for i in range(2):
            total = s.gate_slots[0, i].astype(F32)
            for j in range(1, plane):
                total = total + s.gate_slots[j, i].astype(F32)
            s.gates[which, ha, i] = total
        pltpu.make_async_copy(got, got, s.gate_sems.at[which, 0]).wait()
        mine = s.gates.at[which, ha]
        for z in along_z[1:]:
            pltpu.make_async_remote_copy(
                src_ref=mine, dst_ref=mine, send_sem=s.gate_sems.at[which, 2], recv_sem=s.gate_sems.at[which, 3],
                device_id=(z, wa, img), device_id_type=MESH,
            ).start()

    def gates_wait(which, sem):
        got = s.gates.at[which, pl.ds(0, d.ha - 1)]
        pltpu.make_async_copy(got, got, s.gate_sems.at[which, sem]).wait()

    def img_wait(which, sem):
        got = s.group_x.at[which, pl.ds(0, d.img - 1)]
        pltpu.make_async_copy(got, got, s.group_sems.at[which, sem]).wait()

    def img_start(which, rows_):
        for j, row in enumerate(rows_):
            for i in range(nch):
                line = j * nch + i
                s.group_x[which, img, line : line + 1, :] = row[:, i * LANES : (i + 1) * LANES]
        mine = s.group_x.at[which, img]
        for x in along_img[1:]:
            pltpu.make_async_remote_copy(
                src_ref=mine, dst_ref=mine, send_sem=s.group_sems.at[which, 0], recv_sem=s.group_sems.at[which, 1],
                device_id=(ha, wa, x), device_id_type=MESH,
            ).start()

    def img_finish(which):
        img_wait(which, 1)
        total = s.group_x[which, 0]
        for i in range(1, d.img):
            total = total + s.group_x[which, i]
        s.reduced[0 : 2 * nch, :] = total[0 : 2 * nch]
        return [
            jnp.concatenate([s.reduced[j * nch + i : j * nch + i + 1, :] for i in range(nch)], axis=1)
            for j in range(2)
        ]

    def every(j, k):
        return s.shared[j, :, :, lanes(k)].reshape(n, half)

    def inverse_pixels():
        return spread_lanes(s.invpix[...].reshape(n, LANES), c)

    def excite_forward(j, excitation, sums):
        e = excitation
        pooled = sums * inverse_pixels()
        tiles_start(j, fine(mt if e.turned else mm, pooled, e.down[...]))
        e.pooled[...] = pooled
        before = tiles_finish(j, e.units) + vec(e.down_bias)[:, : e.units]
        e.before[...] = before
        scaling = sigmoid(fine(mm, before * sigmoid(before), e.up[...]) + vec(e.up_bias))
        s.shared[j] = scaling.reshape(d.ha, group, c)

    def excite_backward_start(j, forward, excitation, sums):
        scaling = s.shared[forward].reshape(n, c)
        dlogit = sums * scaling * (1.0 - scaling)
        tiles_start(j, fine(mt, dlogit, excitation.up[...]))
        s.dlogit[...] = dlogit

    def excite_backward(j, excitation, which):
        e = excitation
        before = e.before[...]
        logistic = sigmoid(before)
        dbefore = tiles_finish(j, e.units) * (logistic * (1.0 + before * (1.0 - logistic)))
        dpooled = fine(mm if e.turned else mt, dbefore, e.down[...]) * inverse_pixels()
        img_start(
            which,
            [jnp.sum(dpooled * s.gates[which, :, i].reshape(n, c), axis=0, keepdims=True) for i in range(2)],
        )
        s.shared[j] = dpooled.reshape(d.ha, group, c)
        dlogit = s.dlogit[...]
        s.stage[e.up_at : e.up_at + e.units, :] = exact_tm(before * logistic, dlogit).astype(BF16)
        if e.turned:
            s.stage[e.down_at : e.down_at + e.units, :] = exact_tm(dbefore, e.pooled[...]).astype(BF16)
        else:
            down = exact_tm(e.pooled[...], dbefore)
            for i in range(nch):
                s.stage[e.down_at : e.down_at + LANES, quarter(i)] = down[quarter(i)].astype(BF16)
        owner = jnp.where(here == 0, 1.0, 0.0).astype(F32)
        s.biases[e.bias_at : e.bias_at + 1, :] = jnp.sum(dlogit, axis=0, keepdims=True)
        s.biases[e.bias_at + 1 : e.bias_at + 2, 0 : e.units] = jnp.sum(dbefore, axis=0, keepdims=True) * owner

    one = types.SimpleNamespace(
        turned=True, down=s.squeeze, up=s.excite, units=d.hidden_one, down_bias=SQUEEZE_B, up_bias=EXCITE_B,
        pooled=s.pooled_one, before=s.before_one, down_at=at.squeeze, up_at=at.excite, bias_at=0,
    )
    two = types.SimpleNamespace(
        turned=False, down=s.reduce, up=s.expand, units=d.hidden_two, down_bias=REDUCE_B, up_bias=EXPAND_B,
        pooled=s.pooled_two, before=s.before_two, down_at=at.reduce, up_at=at.expand, bias_at=2,
    )


    class Reduction:
        def __init__(self, index):
            self.index = index
            self.first, self.size = d.jobs[index]
            self.direct = index == 3
            self.hr = self.size if self.direct else self.size // 2
            self.pr = self.hr // d.ha
            self.slot = pl.ds(self.first // (2 * d.ha), self.pr)
            self.mine = self.first if self.direct else self.first + core * self.hr
            self.other = self.first + (1 - core) * self.hr
            self.apart = index >= 2
            self.home = s.excited_two if self.apart else s.stage
            self.shift = d.jobs[2][0] if self.apart else 0

        def sem(self, i):
            return s.grad_sems.at[self.index, i]

        def half_at(self, ref, first):
            return ref.at[pl.ds(pl.multiple_of(first, 16), self.hr)]

        def piece(self, ref, z, y, shift=0):
            first = pl.multiple_of(self.mine - shift + z * self.pr, 16)
            return ref.at[pl.ds(first, self.pr), pl.ds(pl.multiple_of(y * LANES, LANES), LANES)]

        def wait(self, ref, sem):
            pltpu.make_async_copy(ref, ref, self.sem(sem)).wait()

        def swapped(self):
            return s.swaps.at[pl.ds(self.first // 2, self.hr)]

        def many(self):
            return s.scattered.at[pl.ds(0, plane - 1), self.slot]

        def swap(self):
            pltpu.make_async_remote_copy(
                src_ref=self.half_at(s.stage, self.other), dst_ref=self.swapped(), send_sem=self.sem(0),
                recv_sem=self.sem(1), device_id=partner, device_id_type=MESH,
            ).start()

        def scatter(self):
            lines = min(32, self.pr)

            def add(i):
                mine = pl.ds(pl.multiple_of(self.mine + i * lines, 16), lines)
                theirs = pl.ds(pl.multiple_of(self.first // 2 + i * lines, 16), lines)
                s.stage[mine, :] = (s.stage[mine, :].astype(F32) + s.swaps[theirs, :].astype(F32)).astype(BF16)

            if not self.direct:
                self.wait(self.swapped(), 1)
                each_row(add, self.hr // lines)
            for z, y in plane_peers:
                pltpu.make_async_remote_copy(
                    src_ref=self.piece(s.stage, z, y), dst_ref=s.scattered.at[here, self.slot],
                    send_sem=self.sem(2), recv_sem=self.sem(3), device_id=(z, y, img), device_id_type=MESH,
                ).start()
            s.scattered[here, self.slot] = self.piece(s.stage, ha, wa)[...]

        def level(self):
            if self.direct:
                return s.crossed_all, img, d.img, pl.ds(0, self.pr), along_img[1:]
            return s.crossed, chip, chips, self.slot, along_x

        def exchange(self):
            self.wait(self.many(), 3)
            places, own, _, slot, peers = self.level()

            def add(i):
                lines = pl.ds(pl.multiple_of(self.slot.start + i * 16, 16), 16)
                total = s.scattered[0, lines].astype(F32)
                for j in range(1, plane):
                    total = total + s.scattered[j, lines].astype(F32)
                places[own, pl.ds(pl.multiple_of(slot.start + i * 16, 16), 16)] = total.astype(BF16)

            each_row(add, self.pr // 16)
            mine = places.at[own, slot]
            for x in peers:
                pltpu.make_async_remote_copy(
                    src_ref=mine, dst_ref=mine, send_sem=self.sem(4), recv_sem=self.sem(5),
                    device_id=(ha, wa, x), device_id_type=MESH,
                ).start()

        def wait_crossing(self, sem):
            places, _, count, slot, _ = self.level()
            if count > 1:
                self.wait(places.at[pl.ds(0, count - 1), slot], sem)

        def gather(self):
            self.wait_crossing(5)
            places, _, count, slot, _ = self.level()

            def add(i):
                lines = pl.ds(pl.multiple_of(slot.start + i * 16, 16), 16)
                total = places[0, lines].astype(F32)
                for j in range(1, count):
                    total = total + places[j, lines].astype(F32)
                s.summed[pl.ds(pl.multiple_of(self.slot.start + i * 16, 16), 16)] = total.astype(BF16)

            each_row(add, self.pr // 16)
            mine = self.piece(self.home, ha, wa, self.shift)
            mine[...] = s.summed[self.slot]
            for z, y in plane_peers:
                pltpu.make_async_remote_copy(
                    src_ref=s.summed.at[self.slot], dst_ref=mine, send_sem=self.sem(6), recv_sem=self.sem(7),
                    device_id=(z, y, img), device_id_type=MESH,
                ).start()

        def hand(self):
            self.wait(self.many(), 7)
            if self.direct:
                return
            mine = self.half_at(self.home, self.mine - self.shift)
            pltpu.make_async_remote_copy(
                src_ref=mine, dst_ref=mine, send_sem=self.sem(8), recv_sem=self.sem(9),
                device_id=partner, device_id_type=MESH,
            ).start()

        def finish(self):
            if not self.direct:
                self.wait(self.half_at(self.home, self.other - self.shift), 9)
                self.wait(self.half_at(self.home, self.mine - self.shift), 8)
            self.wait(self.many(), 6)
            self.wait_crossing(4)
            if self.apart:
                self.settle()
                lines = min(32, self.size)

                def bring(i):
                    there = pl.ds(pl.multiple_of(self.first + i * lines, 16), lines)
                    here_ = pl.ds(pl.multiple_of(self.first - self.shift + i * lines, 16), lines)
                    s.stage[there, :] = s.excited_two[here_, :]

                each_row(bring, self.size // lines)

        def settle(self):
            self.wait(self.many(), 2)
            if not self.direct:
                self.wait(self.half_at(s.stage, self.other), 0)

    jobs = [Reduction(i) for i in range(len(d.jobs))]


    around = [(dr, dc) for dr in (-1, 0, 1) for dc in (-1, 0, 1) if (dr, dc) != (0, 0)]

    def edge(step):
        if step == 0:
            return pl.ds(1, r_out), pl.ds(1, r_out)
        return (pl.ds(r_out, 1), pl.ds(0, 1)) if step > 0 else (pl.ds(1, 1), pl.ds(r_out + 1, 1))

    def ring_copies(frame, h):
        copies = []
        for i, (dr, dc) in enumerate(around):
            (from_r, to_r), (from_c, to_c) = edge(dr), edge(dc)
            copies.append(
                pltpu.make_async_remote_copy(
                    src_ref=frame.at[from_r, from_c], dst_ref=frame.at[to_r, to_c],
                    send_sem=s.ring_send.at[h, i], recv_sem=s.ring_recv.at[h, i],
                    device_id=beside(dr, dc), device_id_type=MESH,
                )
            )
        return copies

    def three_copies(parts, send, recv):
        return [
            pltpu.make_async_remote_copy(
                src_ref=src, dst_ref=dst, send_sem=send.at[i], recv_sem=recv.at[i],
                device_id=beside(*to), device_id_type=MESH,
            )
            for i, (src, dst, to) in enumerate(parts)
        ]

    def rim_copies():
        last = h_in - 1
        parts = (
            (s.images.at[last], s.rim.at[0], (1, 0)),
            (s.images.at[pl.ds(0, h_in), last], s.rim.at[1], (0, 1)),
            (s.images.at[last, pl.ds(last, 1)], s.rim_corner, (1, 1)),
        )
        return three_copies(parts, s.rim_send, s.rim_recv)

    def corner_copies(frame):
        first, all_, last = pl.ds(0, 1), pl.ds(0, r_out), pl.ds(r_out, 1)
        parts = (
            (frame.at[first, all_], frame.at[last, all_], (-1, 0)),
            (frame.at[all_, first], frame.at[all_, last], (0, -1)),
            (frame.at[first, first], frame.at[last, last], (-1, -1)),
        )
        return three_copies(parts, s.corner_send, s.corner_recv)


    def same_group():
        down = lax.broadcasted_iota(jnp.int32, (half, half), 0) // width
        across = lax.broadcasted_iota(jnp.int32, (half, half), 1) // width
        return jnp.where(down == across, 1.0, 0.0).astype(F32)

    def block_diagonal(source, t, k, same):
        return jnp.concatenate([source[t, :, lanes(k)]] * (half // width), axis=0) * same

    def build_kernel(source):
        same = same_group().astype(BF16)

        def tap(t):
            for k in range(halves):
                s.taps[k, pl.ds(pl.multiple_of(t * half, half), half), :] = block_diagonal(source, t, k, same)

        each_row(tap, 9)

    def build_turned(source, order):
        same = same_group().astype(BF16)
        for i, t in enumerate(order):
            for k in range(halves):
                s.taps[k, i * half : (i + 1) * half, :] = block_diagonal(source, t, k, same).T

    def kernel_grad(dz, window, first):
        down = lax.broadcasted_iota(jnp.int32, (LANES, LANES), 0) // width
        across = lax.broadcasted_iota(jnp.int32, (LANES, LANES), 1) // width
        same = jnp.where(down == across, 1.0, 0.0).astype(F32)
        for q in range(nch):
            s.turned[q] = dz(q).T

        def pair(t):
            taps = [2 * t, jnp.minimum(2 * t + 1, 8)]
            for q in range(nch):
                windows = [window(tap // 3, tap % 3, q) for tap in taps]
                got = mm(s.turned[q], jnp.concatenate(windows, axis=1)).T
                for i, tap in enumerate(taps):
                    block_ = got[i * LANES : (i + 1) * LANES] * same
                    total = block_[0:width]
                    for g in range(1, LANES // width):
                        total = total + block_[g * width : (g + 1) * width]
                    there = pl.ds(pl.multiple_of(first + tap * width, 16), width)
                    s.stage[there, quarter(q)] = total.astype(BF16)

        each_row(pair, 5)

    def product_grad(left, columns, first):
        def some(j):
            span = pl.ds(pl.multiple_of(j * LANES, LANES), LANES)
            got = tm(left(span), s.cot[...].reshape(points, c))
            s.stage[pl.ds(pl.multiple_of(first + j * LANES, 16), LANES), :] = got.astype(BF16)

        each_row(some, columns // LANES)

    def strided(i, ph, pw):
        return jnp.concatenate([s.x[2 * i + ph, 2 * j + pw] for j in range(r_out)], axis=0)

    def bypass(sources, k):
        return mm(sources, s.short_rows[:, lanes(k)])

    def augment(raw, gr, gc):
        mask = mask_at(gr, gc, LANES)
        lane = lax.broadcasted_iota(jnp.int32, (n, ca - ci), 1)
        more = jnp.where(lane < 3, mask[:, : ca - ci], 0.0)
        return jnp.concatenate([raw.astype(F32) * spread_lanes(mask, ci), more], axis=1).astype(BF16)

    def below(value_rows):
        row = lax.broadcasted_iota(jnp.int32, (ca - ci, c), 0)
        total = jnp.zeros((ca - ci, c), F32)
        for i, value in enumerate(value_rows):
            total = jnp.where(row == i, value.astype(F32), total)
        return total

    def gram_moments(gram, kernel_rows):
        parts = in_parts(gram[0:ci, 0:ci], 3)
        product = sum(mm(p, kernel_rows[...]) for p in parts)
        square = jnp.sum(product * kernel_rows[...].astype(F32), axis=0, keepdims=True)
        total = sum(mm(p, kernel_rows[...]) for p in in_parts(gram[ci : ci + 16, 0:ci], 3))[0:1]
        return total, square

    def residual_row(r):
        return s.residual[r + 1, pl.ds(1, r_out)].reshape(block, c)

    def augment(raw, gr, gc):
        mask = mask_at(gr, gc, LANES)
        lane = lax.broadcasted_iota(jnp.int32, (n, ca - ci), 1)
        more = jnp.where(lane < 3, mask[:, : ca - ci], 0.0)
        return jnp.concatenate([raw.astype(F32) * spread_lanes(mask, ci), more], axis=1).astype(BF16)

    def below(value_rows):
        row = lax.broadcasted_iota(jnp.int32, (ca - ci, c), 0)
        total = jnp.zeros((ca - ci, c), F32)
        for i, value in enumerate(value_rows):
            total = jnp.where(row == i, value.astype(F32), total)
        return total

    def gram_moments(gram, kernel_rows):
        parts = in_parts(gram[0:ci, 0:ci], 3)
        product = sum(mm(p, kernel_rows[...]) for p in parts)
        square = jnp.sum(product * kernel_rows[...].astype(F32), axis=0, keepdims=True)
        total = sum(mm(p, kernel_rows[...]) for p in in_parts(gram[ci : ci + 16, 0:ci], 3))[0:1]
        return total, square

    def residual_row(r):
        return s.residual[r + 1, pl.ds(1, r_out)].reshape(block, c)

    def second(r, k):
        return mm(residual_row(r), s.second_kernel[:, lanes(k)])


    depth = s.raw.shape[0]

    def load(h):
        return pltpu.make_async_copy(s.images.at[h], s.raw.at[h % depth], s.load_sems.at[h % depth])

    for h in range(depth):
        load(h).start()
    cot_load = pltpu.make_async_copy(s.cotangent, s.cot, s.cot_sem.at[0])
    cot_load.start()
    vec_loads = [
        pltpu.make_async_copy(getattr(s, name), s.vec.at[i, pl.ds(0, size)], s.vec_sems.at[i])
        for i, (name, size) in enumerate(d.vectors)
    ]
    for copy in vec_loads:
        copy.start()

    barrier = pltpu.get_barrier_semaphore()
    for z, y in plane_peers:
        pl.semaphore_signal(barrier, inc=1, device_id=(z, y, img), device_id_type=MESH)
    for x in along_img[1:]:
        pl.semaphore_signal(barrier, inc=1, device_id=(ha, wa, x), device_id_type=MESH)

    classes = s.classes[...]
    slot = lax.broadcasted_iota(jnp.int32, classes.shape, 1)
    side = 10 + 4 * classes
    index = lax.broadcasted_iota(jnp.int32, classes.shape, 0)
    counts = jnp.zeros(classes.shape, jnp.int32)
    for i in range(d.img):
        counts = jnp.where(index == i, s.image_counts[i], counts)
    cells = jnp.sum(jnp.where(slot < counts, (side * side).astype(F32), 0.0), axis=1, keepdims=True)
    inv_out = 1.0 / jnp.sum(cells, axis=0, keepdims=True)
    inv_in = 0.25 * inv_out
    own_side = (10 + 4 * s.classes[pl.ds(img, 1), :]).astype(F32)
    spread = jnp.broadcast_to(own_side, (n, n))
    diagonal = lax.broadcasted_iota(jnp.int32, (n, n), 0) == lax.broadcasted_iota(jnp.int32, (n, n), 1)
    sides = jnp.sum(jnp.where(diagonal, spread, 0.0), axis=1, keepdims=True)
    sides = jnp.broadcast_to(sides, (n, LANES))
    alive = lax.broadcasted_iota(jnp.int32, (n, LANES), 0) < s.image_counts[img]
    s.lim[...] = jnp.where(alive, 2.0 * sides, 0.0).astype(jnp.int32)
    s.invpix[...] = (1.0 / (sides * sides)).reshape(d.ha, group, LANES)
    s.biases[...] = jnp.zeros((16, c), F32)

    pl.semaphore_wait(barrier, plane - 1 + d.img - 1)
    rims = rim_copies()
    for copy in rims:
        copy.start()

    s.gram[...] = jnp.zeros((ca, ca), F32)
    s.gathered[:, 0:ca] = jnp.zeros((ca, ca), F32)

    def load_rows(i):
        for h in (2 * i, 2 * i + 1):
            load(h).wait()
            for w in range(h_in):
                s.x[h, w] = augment(s.raw[h % depth, w], row0 + h, col0 + w)

            @pl.when(h + depth < h_in)
            def _(h=h):
                load(h + depth).start()

            x = s.x[h].reshape(h_in * n, ca)
            s.gram[...] += tm(x, x)
        x = strided(i, 0, 0)
        s.gathered[:, 0:ca] += tm(x, x)

    each_row(load_rows)
    sums_a = gram_moments(s.gram, s.entry_kernel)
    sum_start(SUM_A, sums_a + gram_moments(s.gathered, s.shortcut_kernel))
    build_kernel(s.group_kernel)
    s.entry_rows[0:ci, :] = s.entry_kernel[...]
    s.short_rows[0:ci, :] = s.shortcut_kernel[...]
    s.short_rows[ci:ca, :] = jnp.zeros((ca - ci, c), BF16)
    for copy in vec_loads:
        copy.wait()
    total_a, square_a, total_s, square_s = sum_finish(SUM_A)
    set_norm(A_, total_a, square_a, inv_in, ENTRY_G, ENTRY_S)
    set_norm(S_, total_s, square_s, inv_out, SHORT_G, SHORT_S)
    raised = vec(ENTRY_S) / keep(A_, 4) - keep(A_, 0)
    s.entry_rows[ci:ca, :] = below(in_parts(raised, 3)).astype(BF16)

    def activate(x, count, store):
        for k in range(halves):
            entry = mm(x, s.entry_rows[:, lanes(k)])
            for j in range(count):
                store(j, k, silu_half(part(entry, j) * keep(A_, 2, k)).astype(BF16))

    def active_row(h):
        for q in range(2):
            def store(j, k, value, q=q):
                s.active[h + 1, 1 + r_out * q + j, :, lanes(k)] = value

            activate(s.x[h, pl.ds(r_out * q, r_out)].reshape(block, ca), r_out, store)

    each_row(active_row, h_in)
    for copy in rims:
        copy.wait_recv()

    for q in range(2):
        def store_top(j, k, value, q=q):
            s.active[0, 1 + r_out * q + j, :, lanes(k)] = value

        def store_left(j, k, value, q=q):
            s.active[1 + r_out * q + j, 0, :, lanes(k)] = value

        for j in range(r_out):
            s.rim_rows[j] = augment(s.rim[0, r_out * q + j], row0 - 1, col0 + r_out * q + j)
        activate(s.rim_rows[...].reshape(block, ca), r_out, store_top)
        for j in range(r_out):
            s.rim_rows[j] = augment(s.rim[1, r_out * q + j], row0 + r_out * q + j, col0 - 1)
        activate(s.rim_rows[...].reshape(block, ca), r_out, store_left)

    def store_corner(j, k, value):
        s.active[0, 0, :, lanes(k)] = value

    activate(augment(s.rim_corner[0], row0 - 1, col0 - 1), 1, store_corner)


    def convolve(window, store):
        def row(r, add):
            masks = masks_out(r)
            for k in range(halves):
                windows = [window(r, ky, kx, k) for ky in range(3) for kx in range(3)]
                field = mm(jnp.concatenate(windows, axis=1), s.taps[k])
                store[rows(r), lanes(k)] = field.astype(BF16)
                for j in range(r_out):
                    masked = part(field, j) * masks[j]
                    add(0, k, masked)
                    add(1, k, masked * part(field, j))

        return over_rows(2, row)

    def window_one(r, ky, kx, k):
        return jnp.concatenate([s.active[2 * r + ky, 2 * j + kx, :, lanes(k)] for j in range(r_out)], axis=0)

    sum_start(SUM_B, convolve(window_one, s.middle))
    build_kernel(s.spatial_kernel)
    set_norm(B_, *sum_finish(SUM_B), inv_out, GROUP_G, GROUP_S)

    def gated(m, store, r, j, k, mask):
        return silu_half(store[spot(r, j), lanes(k)].astype(F32) * keep(m, 2, k) + keep(m, 3, k)) * mask

    def gated_sums(m, store):
        def row(r, add, add_image):
            masks, masks_half = masks_out(r), masks_out(r, 0.5)
            for j, k in pieces:
                field = store[spot(r, j), lanes(k)].astype(F32)
                value, slope = silu_and_slope(field * keep(m, 2, k) + keep(m, 3, k))
                slope = slope * masks_half[j]
                add_image(0, k, value * masks[j])
                add_image(1, k, slope)
                add_image(2, k, slope * field)

        return over(0, 3, row)

    def excite_row(r, m, store, forward, excited):
        masks = masks_out(r)
        for j, k in pieces:
            value = gated(m, store, r, j, k, masks[j]) * every(forward, k)
            excited[spot(r, j), lanes(k)] = value.astype(BF16)

    pooled_sums, *gate_sums = gated_sums(B_, s.middle)
    excite_forward(0, one, pooled_sums)
    gates_load(gate_sums)

    def branch_row(r, add):
        excite_row(r, B_, s.middle, 0, s.excited_one)
        for k in range(halves):
            field = mm(s.excited_one[rows(r), :], s.output_kernel[:, lanes(k)])
            s.branch[rows(r), lanes(k)] = field.astype(BF16)
            add(0, k, field)
            add(1, k, field * field)

    sum_start(SUM_C, over_rows(2, branch_row))
    set_norm(C_, *sum_finish(SUM_C), inv_out, OUTPUT_G, OUTPUT_S)


    def total_one_half(field, skip, k):
        return field * keep(C_, 2, k) + skip * keep(S_, 2, k) + (keep(C_, 3, k) + keep(S_, 3, k))

    def second_row(r, add):
        masks, sources = masks_out(r), strided(r, 0, 0)
        for k in range(halves):
            skip = bypass(sources, k)
            for j in range(r_out):
                field = s.branch[spot(r, j), lanes(k)].astype(F32)
                value = silu_half(total_one_half(field, part(skip, j), k)) * masks[j]
                s.residual[r + 1, 1 + j, :, lanes(k)] = value.astype(BF16)
        for k in range(halves):
            field = mm(residual_row(r), s.second_kernel[:, lanes(k)])
            s.second[rows(r), lanes(k)] = field.astype(BF16)
            add(0, k, field)
            add(1, k, field * field)

    sums_d = over_rows(2, second_row)
    ring = ring_copies(s.residual, 0)
    for copy in ring:
        copy.start()
    sum_start(SUM_D, sums_d)
    s.square_t[...] = s.final_kernel[...].T
    set_norm(D_, *sum_finish(SUM_D), inv_out, SECOND_G, SECOND_S)
    gates_start(0)

    def put_active_two(field, fr, fc, k):
        mask = mask_at(row0 + 2 * (fr - 1), col0 + 2 * (fc - 1), half)
        value = silu_half(field * keep(D_, 2, k) + keep(D_, 3, k)) * mask
        s.frame[fr, fc, :, lanes(k)] = value.astype(BF16)

    def active_two(x, places):
        for k in range(halves):
            field = mm(x, s.second_kernel[:, lanes(k)])
            for j, (fr, fc) in enumerate(places):
                put_active_two(part(field, j), fr, fc, k)

    def active_two_row(r):
        for j, k in pieces:
            put_active_two(s.second[spot(r, j), lanes(k)].astype(F32), r + 1, 1 + j, k)

    each_row(active_two_row)
    for copy in ring:
        copy.wait_recv()
    for fr in (0, r_out + 1):
        x = s.residual[fr].reshape((r_out + 2) * n, c)
        active_two(x, [(fr, fc) for fc in range(r_out + 2)])
    for fc in (0, r_out + 1):
        x = s.residual[pl.ds(1, r_out), fc].reshape(block, c)
        active_two(x, [(fr, fc) for fr in range(1, r_out + 1)])

    def window_two(r, ky, kx, k):
        return s.frame[r + ky, pl.ds(kx, r_out), :, lanes(k)].reshape(block, half)

    sum_start(SUM_E, convolve(window_two, s.spatial))
    s.start_rows[0:c, :] = s.shortcut_kernel[...].T
    gates_finish(0)
    set_norm(E_, *sum_finish(SUM_E), inv_out, SPATIAL_G, SPATIAL_S)

    pooled_sums, *gate_sums = gated_sums(E_, s.spatial)
    excite_forward(1, two, pooled_sums)
    gates_load(gate_sums)

    def final_row(r, add):
        excite_row(r, E_, s.spatial, 1, s.excited_two)
        for k in range(halves):
            field = mm(s.excited_two[rows(r), :], s.final_kernel[:, lanes(k)])
            s.field[rows(r), lanes(k)] = field
            add(0, k, field)
            add(1, k, field * field)

    sum_start(SUM_F, over_rows(2, final_row))
    cot_load.wait()
    build_turned(s.spatial_kernel, range(9))
    set_norm(F_, *sum_finish(SUM_F), inv_out, FINAL_G, FINAL_S)
    gates_start(1)


    def top_row(r, add):
        masks, masks_half = masks_out(r), masks_out(r, 0.5)
        for j, k in pieces:
            field = s.field[spot(r, j), lanes(k)]
            kept = s.residual[r + 1, 1 + j, :, lanes(k)].astype(F32)
            value, slope = silu_and_slope(field * keep(F_, 2, k) + keep(F_, 3, k) + 0.5 * kept)
            upstream = s.cot[r, j, :, lanes(k)].astype(F32) * masks_half[j] * slope
            s.cot[r, j, :, lanes(k)] = (value * masks[j]).astype(BF16)
            s.upstream[spot(r, j), lanes(k)] = upstream
            add(0, k, upstream)
            add(1, k, upstream * field)

    sum_start(BACK_F, over_rows(2, top_row))
    gates_finish(1)
    activations_out = pltpu.make_async_copy(s.cot, s.activations, s.cot_sem.at[1])
    activations_out.start()
    set_back(F_, *sum_finish(BACK_F), inv_out, FINAL_G)
    activations_out.wait()

    def excited_back(r, add, add_image, m, store, forward):
        masks, masks_half = masks_out(r), masks_out(r, 0.5)
        dz = s.cot[r].reshape(block, c)
        for k in range(halves):
            dexcited = mm(dz, s.square_t[:, lanes(k)])
            s.field[rows(r), lanes(k)] = dexcited
            for j in range(r_out):
                field = store[spot(r, j), lanes(k)].astype(F32)
                value, slope = silu_and_slope(field * keep(m, 2, k) + keep(m, 3, k))
                add_image(0, k, part(dexcited, j) * (value * masks[j]))
                upstream = part(dexcited, j) * every(forward, k) * (slope * masks_half[j])
                add(0, k, upstream)
                add(1, k, upstream * field)

    def final_back(r, add, add_image):
        masks = masks_out(r)
        for j, k in pieces:
            upstream, field = s.upstream[spot(r, j), lanes(k)], s.field[spot(r, j), lanes(k)]
            s.cot[r, j, :, lanes(k)] = back(F_, upstream, field, masks[j], k)
        excited_back(r, add, add_image, E_, s.spatial, 1)

    *sums_e, dscaling_sums = over(2, 1, final_back)
    excite_backward_start(2, 1, two, dscaling_sums)
    sum_start(BACK_E, sums_e)
    product_grad(lambda span: s.excited_two[0:points, span], c, at.final)
    gates_wait(1, 3)
    excite_backward(2, two, 1)

    def gate_back(m, forward, backward, store, put):
        def row(r):
            masks, masks_half = masks_out(r), masks_out(r, 0.5)
            for j, k in pieces:
                field = store[spot(r, j), lanes(k)].astype(F32)
                _, slope = silu_and_slope(field * keep(m, 2, k) + keep(m, 3, k))
                dgated = s.field[spot(r, j), lanes(k)] * every(forward, k) + every(backward, k)
                put(r, j, k, back(m, dgated * masks_half[j] * slope, field, masks[j], k))

        each_row(row)

    def finish_gate(k, which):
        shift_sum, weighted = sum_finish(k)
        more_shift, more_weighted = img_finish(which)
        return shift_sum + more_shift, weighted + more_weighted

    set_back(E_, *finish_gate(BACK_E, 1), inv_out, SPATIAL_G)

    def put_spatial(r, j, k, dz):
        s.dframe[r + 1, 1 + j, :, lanes(k)] = dz

    gate_back(E_, 1, 2, s.spatial, put_spatial)
    ring_back = ring_copies(s.dframe, 1)
    for copy in ring_back:
        copy.start()
    inner = pl.ds(1, r_out)
    outer = pl.ds(0, r_out)

    def all_two(ky, kx, q):
        return s.frame[pl.ds(ky, r_out), pl.ds(kx, r_out), :, quarter(q)].reshape(points, LANES)

    kernel_grad(lambda q: s.dframe[inner, inner, :, quarter(q)].reshape(points, LANES), all_two, at.spatial)
    for copy in ring_back:
        copy.wait_recv()
    blank = jnp.zeros((r_out + 2, n, c), BF16)

    @pl.when(ha == 0)
    def _():
        s.dframe[0] = blank

    @pl.when(ha == d.ha - 1)
    def _():
        s.dframe[r_out + 1] = blank

    @pl.when(wa == 0)
    def _():
        s.dframe[:, 0] = blank

    @pl.when(wa == d.wa - 1)
    def _():
        s.dframe[:, r_out + 1] = blank

    def second_back(r, add):
        masks = masks_out(r, 0.5)
        for k in range(halves):
            windows = [
                s.dframe[r + 2 - ky, pl.ds(2 - kx, r_out), :, lanes(k)].reshape(block, half)
                for ky in range(3)
                for kx in range(3)
            ]
            total = mm(jnp.concatenate(windows, axis=1), s.taps[k])
            for j in range(r_out):
                field = s.second[spot(r, j), lanes(k)].astype(F32)
                _, slope = silu_and_slope(field * keep(D_, 2, k) + keep(D_, 3, k))
                upstream = part(total, j) * masks[j] * slope
                s.field[spot(r, j), lanes(k)] = upstream
                add(0, k, upstream)
                add(1, k, upstream * field)

    sum_start(BACK_D, over_rows(2, second_back))
    jobs[0].swap()
    build_turned(s.group_kernel, PARITY_TAPS)
    s.square_t[...] = s.second_kernel[...].T
    set_back(D_, *sum_finish(BACK_D), inv_out, SECOND_G)


    def residual_back(r, add):
        masks, masks_half, sources = masks_out(r), masks_out(r, 0.5), strided(r, 0, 0)
        for j, k in pieces:
            upstream, field = s.field[spot(r, j), lanes(k)], s.second[spot(r, j), lanes(k)].astype(F32)
            s.cot[r, j, :, lanes(k)] = back(D_, upstream, field, masks[j], k)
        dz = s.cot[r].reshape(block, c)
        for k in range(halves):
            dresidual, skips = mm(dz, s.square_t[:, lanes(k)]), bypass(sources, k)
            for j in range(r_out):
                field, skip = s.branch[spot(r, j), lanes(k)].astype(F32), part(skips, j)
                _, slope = silu_and_slope(total_one_half(field, skip, k))
                upstream = (s.upstream[spot(r, j), lanes(k)] + part(dresidual, j)) * masks_half[j] * slope
                s.field[spot(r, j), lanes(k)] = upstream
                add(0, k, upstream)
                add(1, k, upstream * field)
                add(2, k, upstream * skip)

    sum_start(BACK_C, over_rows(3, residual_back))
    product_grad(lambda span: s.residual[inner, inner, :, span].reshape(points, LANES), c, at.second)
    jobs[0].scatter()
    s.square_t[...] = s.output_kernel[...].T
    shift_c, gain_c, gain_s = sum_finish(BACK_C)
    set_back(C_, shift_c, gain_c, inv_out, OUTPUT_G)
    set_back(S_, shift_c, gain_s, inv_out, SHORT_G)

    s.gathered[...] = jnp.zeros((ca, c), F32)

    def branch_back(r, add, add_image):
        masks, sources = masks_out(r), strided(r, 0, 0)
        for k in range(halves):
            skips = bypass(sources, k)
            for j in range(r_out):
                upstream, field = s.field[spot(r, j), lanes(k)], s.branch[spot(r, j), lanes(k)].astype(F32)
                s.cot[r, j, :, lanes(k)] = back(C_, upstream, field, masks[j], k)
                s.skip[j * n : (j + 1) * n, lanes(k)] = back(S_, upstream, part(skips, j), masks[j], k)
        s.gathered[...] += tm(sources, s.skip[...])
        s.upstream[rows(r), 0:ci] = mm(s.skip[...], s.start_rows[0:c, :])
        excited_back(r, add, add_image, B_, s.middle, 0)

    *sums_b, dscaling_sums = over(2, 1, branch_back)
    jobs[0].settle()
    excite_backward_start(3, 0, one, dscaling_sums)
    sum_start(BACK_B, sums_b)
    s.stage[at.shortcut : at.shortcut + ci, :] = s.gathered[0:ci, :].astype(BF16)
    product_grad(lambda span: s.excited_one[:, span], c, at.output)
    jobs[0].exchange()
    gates_wait(0, 3)
    excite_backward(3, one, 0)
    s.stage[at.biases : at.biases + 16, :] = s.biases[...].astype(BF16)
    jobs[0].gather()
    jobs[1].swap()
    set_back(B_, *finish_gate(BACK_B, 0), inv_out, GROUP_G)

    def put_middle(r, j, k, dz):
        s.frame[r, j, :, lanes(k)] = dz

    gate_back(B_, 0, 3, s.middle, put_middle)
    corners = corner_copies(s.frame)
    for copy in corners:
        copy.start()

    def all_one(ky, kx, q):
        return jnp.concatenate(
            [s.active[2 * i + ky, 2 * j + kx, :, quarter(q)] for i in range(r_out) for j in range(r_out)], axis=0
        )

    kernel_grad(lambda q: s.frame[outer, outer, :, quarter(q)].reshape(points, LANES), all_one, at.group)
    jobs[0].hand()
    jobs[1].scatter()
    jobs[2].swap()
    for copy in corners:
        copy.wait_recv()

    @pl.when(ha == d.ha - 1)
    def _():
        s.frame[r_out] = blank

    @pl.when(wa == d.wa - 1)
    def _():
        s.frame[:, r_out] = blank

    meets = {0: ((1, 0),), 1: ((0, 1), (2, 0))}
    parities = [(ph, pw) for ph in range(2) for pw in range(2)]

    def entry_sums(i, add):
        for ph, pw in parities:
            first, last = PARITY_SPANS[ph, pw]
            sources = strided(i, ph, pw)
            for k in range(halves):
                windows = [
                    s.frame[i + dr, pl.ds(dc, r_out), :, lanes(k)].reshape(block, half)
                    for _, dr in meets[ph]
                    for _, dc in meets[pw]
                ]
                window = windows[0] if len(windows) == 1 else jnp.concatenate(windows, axis=1)
                dactive = mm(window, s.taps[k, first * half : last * half, :])
                fields = mm(sources, s.entry_rows[:, lanes(k)])
                for j in range(r_out):
                    field = part(fields, j)
                    _, slope = silu_and_slope(field * keep(A_, 2, k))
                    mask = mask_at(row0 + 2 * i + ph, col0 + 2 * j + pw, half, 0.5)
                    upstream = part(dactive, j) * mask * slope
                    s.active[2 * i + ph + 1, 2 * j + pw + 1, :, lanes(k)] = upstream.astype(BF16)
                    add(0, k, upstream)
                    add(1, k, upstream * field)

    sums_e = over_rows(2, entry_sums)
    jobs[1].settle()
    sum_start(BACK_A, sums_e)
    jobs[1].exchange()
    jobs[2].scatter()
    s.gathered[...] = jnp.zeros((ca, c), F32)

    def meet(h):
        upstream = s.active[h + 1, pl.ds(1, h_in)].reshape(h_in * n, c)
        s.gathered[...] += tm(s.x[h].reshape(h_in * n, ca), upstream)

    each_row(meet, h_in)
    set_back(A_, *sum_finish(BACK_A), inv_in, ENTRY_G, raised)

    kernel_rows = s.entry_kernel[...].astype(F32)
    folded = jnp.concatenate([kernel_rows * keep(A_, 6), below([keep(A_, 7)])], axis=0)
    s.stage[at.entry : at.entry + ci, :] = (
        s.gathered[0:ci, :] * keep(A_, 5) + exact(mm, s.gram[0:ci, :], folded)
    ).astype(BF16)
    jobs[3].scatter()
    s.start_rows[0:c, :] = (kernel_rows * keep(A_, 5)).T.astype(BF16)
    high, low = in_parts(fine(mt, folded, s.entry_kernel[...]), 2)
    s.start_rows[c : c + ca, :] = high
    s.start_rows[c + ca : c + 2 * ca, :] = low
    jobs[1].gather()
    jobs[2].exchange()

    def store_row(h):
        return pltpu.make_async_copy(s.raw.at[h % depth], s.images_grad.at[h], s.load_sems.at[h % depth])

    def start_back(i):
        for ph in range(2):
            h = 2 * i + ph

            @pl.when(h >= depth)
            def _(h=h):
                store_row(h - depth).wait()

            for q in range(2):
                span = pl.ds(r_out * q, r_out)
                upstream = s.active[h + 1, pl.ds(1 + r_out * q, r_out)].reshape(block, c)
                x = s.x[h, span].reshape(block, ca)
                dstart = mm(jnp.concatenate([upstream, x, x], axis=1), s.start_rows[...])
                for j in range(r_out):
                    w = r_out * q + j
                    value = part(dstart, j)
                    if ph == 0 and w % 2 == 0:
                        value = value + s.upstream[spot(i, w // 2), 0:ci]
                    s.raw[h % depth, w] = value.astype(BF16)
            store_row(h).start()

    each_row(start_back, 2)
    jobs[3].exchange()
    jobs[1].hand()
    jobs[2].gather()
    each_row(start_back, r_out, 2)
    jobs[3].gather()
    jobs[2].hand()
    jobs[3].hand()


    for copy in rims + ring + ring_back + corners:
        copy.wait_send()
    for k in range(len(VECTORS)):
        sum_wait(k, 0)
        sum_wait_across(k, 2)
    for j in range(4):
        tiles_wait(j, 0)
    for which in range(2):
        gates_wait(which, 2)
        img_wait(which, 0)
    for h in range(h_in - depth, h_in):
        store_row(h).wait()
    for job in jobs:
        job.finish()


def run(d, operands):
    n, c, ci, r = d.images, d.channels, d.inputs, d.rows
    points, h_in, group = r * r * n, 2 * r, n // d.ha
    plane = d.ha * d.wa
    half = min(256, c)
    vm = functools.partial(pl.BlockSpec, memory_space=pltpu.VMEM)
    anywhere = functools.partial(pl.BlockSpec, memory_space=pl.ANY)
    smem = functools.partial(pl.BlockSpec, memory_space=pltpu.SMEM)
    inputs = dict(
        images=anywhere(), cotangent=anywhere(), classes=vm(), image_counts=smem(),
        **{name: anywhere() for name, _ in d.vectors},
        entry_kernel=vm(), group_kernel=vm(), squeeze=vm(), excite=vm(), output_kernel=vm(), shortcut_kernel=vm(),
        second_kernel=vm(), spatial_kernel=vm(), reduce=vm(), expand=vm(), final_kernel=vm(),
    )
    outputs = dict(
        activations=(jax.ShapeDtypeStruct((r, r, n, c), BF16), anywhere()),
        images_grad=(jax.ShapeDtypeStruct((h_in, h_in, n, ci), BF16), anywhere()),
        stage=(jax.ShapeDtypeStruct((d.grad_lines, c), BF16), vm()),
        vectors=(jax.ShapeDtypeStruct((16, c), F32), vm()),
    )
    dma = pltpu.SemaphoreType.DMA
    narrow = -(-2 * (c // LANES) // 8) * 8
    last = d.jobs[3][1] // d.ha
    sums, lines = len(VECTORS), d.grad_lines // (2 * d.ha) + last // 2
    scratch = dict(
        x=pltpu.VMEM((h_in, h_in, n, d.augmented), BF16),
        raw=pltpu.VMEM((2, h_in, n, ci), BF16),
        rim=pltpu.VMEM((2, h_in, n, ci), BF16),
        rim_corner=pltpu.VMEM((1, n, ci), BF16),
        rim_rows=pltpu.VMEM((r, n, d.augmented), BF16),
        active=pltpu.VMEM((h_in + 1, h_in + 1, n, c), BF16),
        cot=pltpu.VMEM((r, r, n, c), BF16),
        middle=pltpu.VMEM((points, c), BF16),
        branch=pltpu.VMEM((points, c), BF16),
        second=pltpu.VMEM((points, c), BF16),
        excited_one=pltpu.VMEM((points, c), BF16),
        residual=pltpu.VMEM((r + 2, r + 2, n, c), BF16),
        frame=pltpu.VMEM((r + 2, r + 2, n, c), BF16),
        spatial=pltpu.VMEM((points, c), BF16),
        excited_two=pltpu.VMEM((max(points, d.grad_lines - d.jobs[2][0]), c), BF16),
        field=pltpu.VMEM((points, c), F32),
        upstream=pltpu.VMEM((points, c), F32),
        dframe=pltpu.VMEM((r + 2, r + 2, n, c), BF16),
        skip=pltpu.VMEM((r * n, c), BF16),
        turned=pltpu.VMEM((c // LANES, LANES, points), BF16),
        taps=pltpu.VMEM((c // half, 9 * half, half), BF16),
        entry_rows=pltpu.VMEM((d.augmented, c), BF16),
        short_rows=pltpu.VMEM((d.augmented, c), BF16),
        start_rows=pltpu.VMEM((c + 2 * d.augmented, ci), BF16),
        gram=pltpu.VMEM((d.augmented, d.augmented), F32),
        square_t=pltpu.VMEM((c, c), BF16),
        gathered=pltpu.VMEM((d.augmented, c), F32),
        biases=pltpu.VMEM((16, c), F32),
        vec=pltpu.VMEM((24, c), F32),
        lim=pltpu.VMEM((n, LANES), jnp.int32),
        invpix=pltpu.VMEM((d.ha, group, LANES), F32),
        keep=pltpu.VMEM((56, c), F32),
        slots=pltpu.VMEM((sums, plane, narrow, LANES), F32),
        across=pltpu.VMEM((sums, d.img, narrow, LANES), F32),
        slots_wide=pltpu.VMEM((2, plane, 2 * narrow, LANES), F32),
        across_wide=pltpu.VMEM((2, d.img, 2 * narrow, LANES), F32),
        reduced=pltpu.VMEM((16, LANES), F32),
        tile_slots=pltpu.VMEM((4, plane, n, LANES), BF16),
        dlogit=pltpu.VMEM((n, c), F32),
        gate_src=pltpu.VMEM((d.ha, 2, group, c), BF16),
        gate_slots=pltpu.VMEM((plane, 2, group, c), BF16),
        shared=pltpu.VMEM((4, d.ha, group, c), F32),
        gates=pltpu.VMEM((2, d.ha, 2, group, c), F32),
        group_x=pltpu.VMEM((2, d.img, narrow, LANES), F32),
        pooled_one=pltpu.VMEM((n, c), F32),
        before_one=pltpu.VMEM((n, d.hidden_one), F32),
        pooled_two=pltpu.VMEM((n, c), F32),
        before_two=pltpu.VMEM((n, d.hidden_two), F32),
        swaps=pltpu.VMEM((d.grad_lines // 2, c), BF16),
        scattered=pltpu.VMEM((plane, lines, LANES), BF16),
        crossed=pltpu.VMEM((d.img // 2, lines, LANES), BF16),
        crossed_all=pltpu.VMEM((d.img, last, LANES), BF16),
        summed=pltpu.VMEM((lines, LANES), BF16),
        load_sems=dma((2,)),
        vec_sems=dma((len(d.vectors),)),
        cot_sem=dma((2,)),
        sum_sems=dma((sums, 4)),
        tile_sems=dma((4, 2)),
        gate_sems=dma((2, 4)),
        group_sems=dma((2, 2)),
        ring_send=dma((2, 8)),
        ring_recv=dma((2, 8)),
        rim_send=dma((3,)),
        rim_recv=dma((3,)),
        corner_send=dma((3,)),
        corner_recv=dma((3,)),
        grad_sems=dma((len(d.jobs), 10)),
    )
    d.names = [*inputs, *outputs, *scratch]
    return pl.pallas_call(
        functools.partial(kernel, d),
        out_shape=[shape for shape, _ in outputs.values()],
        in_specs=list(inputs.values()),
        out_specs=[spec for _, spec in outputs.values()],
        scratch_shapes=list(scratch.values()),
        compiler_params=pltpu.CompilerParams(
            collective_id=0, has_side_effects=True, vmem_limit_bytes=d.vmem, fuse_transposed_lhs_in_matmul=True
        ),
        name="blocks",
    )(*[operands[name] for name in inputs])


def widen(d, activations, images_grad, total, sums):
    names = [name for name, (_, size) in d.grad_rows.items() if size != 16]
    first_bias = [first for first, size in d.grad_rows.values() if size == 16][0]
    c, nch = d.channels, d.channels // LANES
    vectors = sums.shape[0]
    bias_sizes = (c, LANES, c, LANES)

    def shape_of(name):
        return (c, d.hidden_two) if name == d.chunked else (d.grad_rows[name][1], c)

    def widen_kernel(activations_in, images_in, total_in, sums_in, *refs):
        outs, (large_a, large_b, biases, sems, vec_sems) = refs[:-5], refs[-5:]
        activations_out, images_out, *rest = outs
        grads, lines = rest[: len(names)], rest[len(names) :]
        arriving = [
            pltpu.make_async_copy(images_in, large_a, sems.at[0]),
            pltpu.make_async_copy(activations_in, large_b, sems.at[1]),
        ]
        leaving = [
            pltpu.make_async_copy(large_a, images_out, sems.at[2]),
            pltpu.make_async_copy(large_b, activations_out, sems.at[3]),
        ]
        for copy in arriving:
            copy.start()
        biases[...] = total_in[first_bias : first_bias + 16, :].astype(F32)
        sources = [sums_in.at[i] for i in range(vectors)]
        sources += [biases.at[i, pl.ds(0, size)] for i, size in enumerate(bias_sizes)]
        small = [
            pltpu.make_async_copy(source, line, vec_sems.at[i])
            for i, (source, line) in enumerate(zip(sources, lines, strict=True))
        ]
        for copy in small:
            copy.start()
        for into, out in zip(arriving, leaving, strict=True):
            into.wait()
            out.start()
        for name, out in zip(names, grads, strict=True):
            first, size = d.grad_rows[name]
            if name == d.chunked:
                for i in range(nch):
                    chunk = total_in[first : first + size, i * LANES : (i + 1) * LANES]
                    out[i * LANES : (i + 1) * LANES, :] = chunk.astype(F32)
            else:
                out[...] = total_in[first : first + size, :].astype(F32)
        for copy in small + leaving:
            copy.wait()

    anywhere = pl.BlockSpec(memory_space=pl.ANY)
    inside = pl.BlockSpec(memory_space=pltpu.VMEM)
    line_sizes = (c,) * vectors + bias_sizes
    out = pl.pallas_call(
        widen_kernel,
        out_shape=[
            jax.ShapeDtypeStruct(activations.shape, BF16), jax.ShapeDtypeStruct(images_grad.shape, BF16),
            *[jax.ShapeDtypeStruct(shape_of(name), F32) for name in names],
            *[jax.ShapeDtypeStruct((size,), F32) for size in line_sizes],
        ],
        in_specs=[anywhere, anywhere, inside, inside],
        out_specs=[anywhere, anywhere, *[inside] * len(names), *[anywhere] * len(line_sizes)],
        scratch_shapes=[
            pltpu.VMEM(images_grad.shape, BF16), pltpu.VMEM(activations.shape, BF16), pltpu.VMEM((16, c), F32),
            pltpu.SemaphoreType.DMA((4,)), pltpu.SemaphoreType.DMA((len(line_sizes),)),
        ],
        compiler_params=pltpu.CompilerParams(vmem_limit_bytes=d.vmem),
        name="widen",
    )(activations, images_grad, total, sums)
    grads, lines = out[2 : 2 + len(names)], out[2 + len(names) :]
    return out[0], out[1], types.SimpleNamespace(**dict(zip(names, grads, strict=True))), lines


def body(
    images, classes, image_counts, entry_kernel, entry_gain, entry_shift, group_kernel, group_gain, group_shift,
    squeeze_weight, squeeze_bias, excite_weight, excite_bias, output_kernel, output_gain, output_shift,
    shortcut_kernel, shortcut_gain, shortcut_shift, second_kernel, second_gain, second_shift, spatial_kernel,
    spatial_gain, spatial_shift, reduce_weight, reduce_bias, expand_weight, expand_bias, final_kernel, final_gain,
    final_shift, cotangent,
):
    vectors = dict(
        entry_gain=entry_gain, entry_shift=entry_shift, group_gain=group_gain, group_shift=group_shift,
        output_gain=output_gain, output_shift=output_shift, shortcut_gain=shortcut_gain,
        shortcut_shift=shortcut_shift, second_gain=second_gain, second_shift=second_shift,
        spatial_gain=spatial_gain, spatial_shift=spatial_shift, final_gain=final_gain, final_shift=final_shift,
        excite_bias=excite_bias, expand_bias=expand_bias,
        squeeze_bias=jnp.pad(squeeze_bias, (0, -squeeze_bias.shape[0] % LANES)), reduce_bias=reduce_bias,
    )
    d = types.SimpleNamespace(
        ha=lax.axis_size("ha"), wa=lax.axis_size("wa"), img=lax.axis_size("img"),
        images=images.shape[0], rows=images.shape[1] // 2, inputs=images.shape[3],
        channels=entry_kernel.shape[1], width=group_kernel.shape[2],
        hidden_one=squeeze_weight.shape[1], hidden_two=reduce_weight.shape[1], vmem=64 * 1024 * 1024 - 65536,
        vectors=[(name, v.shape[0]) for name, v in vectors.items()],
    )
    n, c = d.images, d.channels
    d.grad_rows, d.jobs, d.grad_lines = grad_rows(c, d.inputs, d.hidden_one, d.hidden_two, d.width)
    d.augmented = -(-(d.inputs + 3) // LANES) * LANES
    d.chunked = list(d.grad_rows)[1]
    operands = dict(
        **vectors,
        images=images.transpose(1, 2, 0, 3),
        cotangent=cotangent.transpose(1, 2, 0, 3),
        classes=classes.reshape(d.img, n),
        image_counts=image_counts,
        entry_kernel=entry_kernel,
        group_kernel=group_kernel.reshape(9, d.width, c),
        squeeze=squeeze_weight.T,
        excite=excite_weight,
        output_kernel=output_kernel,
        shortcut_kernel=shortcut_kernel,
        second_kernel=second_kernel,
        spatial_kernel=spatial_kernel.reshape(9, d.width, c),
        reduce=reduce_weight,
        expand=expand_weight,
        final_kernel=final_kernel,
    )
    activations, images_grad, total, sums = run(d, operands)
    activations, images_grad, g, lines = widen(d, activations, images_grad, total, sums)
    biases = lines[-4:]

    def taps_of(v):
        return v.reshape(3, 3, d.width, c)

    def pair(i):
        return lines[i], lines[i + 1]

    return (
        activations.transpose(2, 0, 1, 3),
        images_grad.transpose(2, 0, 1, 3),
        g.entry, *pair(ENTRY_G),
        taps_of(g.group), *pair(GROUP_G),
        g.squeeze.T, biases[1][: d.hidden_one], g.excite, biases[0],
        g.output, *pair(OUTPUT_G),
        g.shortcut, *pair(SHORT_G),
        g.second, *pair(SECOND_G),
        taps_of(g.spatial), *pair(SPATIAL_G),
        g.reduce, biases[3][: d.hidden_two], g.expand, biases[2],
        g.final, *pair(FINAL_G),
    )


def solution(mesh):
    spread = P("img", "ha", "wa", None)
    return jax.shard_map(
        body,
        mesh=mesh,
        in_specs=(spread, *[P()] * 31, spread),
        out_specs=(spread, spread, *[P()] * 29),
        check_vma=False,
    )
```

```python
import functools
import types

import jax
import jax.numpy as jnp
from jax import lax
from jax.experimental import pallas as pl
from jax.experimental.pallas import tpu as pltpu
from jax.sharding import PartitionSpec as P

EPS = 1e-05
F32 = jnp.float32
BF16 = jnp.bfloat16
MESH = pl.DeviceIdType.MESH
FAR = 1 << 20
LANES = 128
SENT = "_sent"

(
    ENTRY_G, ENTRY_S, GROUP_G, GROUP_S, OUTPUT_G, OUTPUT_S, SHORT_G, SHORT_S, SECOND_G, SECOND_S,
    SPATIAL_G, SPATIAL_S, FINAL_G, FINAL_S, EXCITE_B, EXPAND_B, SQUEEZE_B, REDUCE_B,
) = range(18)

A_, S_, B_, C_, D_, E_, F_ = range(7)
(SUM_A, SUM_B, SUM_C, SUM_D, SUM_E, SUM_F, BACK_F, BACK_E, BACK_D, BACK_C, BACK_B, BACK_A) = range(12)
VECTORS = (4, 2, 2, 2, 2, 2, 2, 2, 2, 3, 2, 2)

PARITY_TAPS = (4, 3, 5, 1, 7, 0, 2, 6, 8)
PARITY_SPANS = {(0, 0): (0, 1), (0, 1): (1, 3), (1, 0): (3, 5), (1, 1): (5, 9)}


def mm(a, b):
    return lax.dot_general(a, b, (((1,), (0,)), ((), ())), preferred_element_type=F32)


def mt(a, b):
    return lax.dot_general(a, b, (((1,), (1,)), ((), ())), preferred_element_type=F32)


def tm(a, b):
    return lax.dot_general(a, b, (((0,), (0,)), ((), ())), preferred_element_type=F32)


def exact_tm(a, b):
    return lax.dot_general(
        a, b, (((0,), (0,)), ((), ())), precision=lax.Precision.HIGHEST, preferred_element_type=F32
    )


def split_rows(a):
    high = a.astype(BF16)
    return jnp.concatenate([high, (a - high.astype(F32)).astype(BF16)], axis=0)


def fine(product, a, b):
    both = product(split_rows(a), b)
    return both[: a.shape[0]] + both[a.shape[0] :]


def fold(v):
    return jnp.sum(v.reshape(v.shape[0] // 8, 8, v.shape[1]), axis=0)


def sigmoid(v):
    return 0.5 * jnp.tanh(0.5 * v) + 0.5


def silu_half(y):
    return y * jnp.tanh(y) + y


def silu_and_slope(y):
    t = jnp.tanh(y)
    u = y * t
    return y + u, (1.0 + t) * (1.0 + (y - u))


def in_parts(v, count):
    parts = []
    for _ in range(count):
        parts.append(v.astype(BF16))
        v = v - parts[-1].astype(F32)
    return parts


def exact(product, a, b):
    (a_high, a_low), (b_high, b_low) = in_parts(a, 2), in_parts(b, 2)
    return product(a_high, b_high) + (product(a_low, b_high) + product(a_high, b_low))


def spread_lanes(m, width):
    whole, rest = divmod(width, LANES)
    parts = [m] * whole + ([m[:, :rest]] if rest else [])
    return parts[0] if len(parts) == 1 else jnp.concatenate(parts, axis=1)


def grad_rows(channels, inputs, hidden_one, hidden_two, width):
    groups = (
        dict(final=channels, reduce=hidden_two, expand=hidden_two, spatial=9 * width),
        dict(
            second=channels, output=channels, shortcut=inputs, squeeze=hidden_one, excite=hidden_one, biases=16
        ),
        dict(group=9 * width),
        dict(entry=inputs),
    )
    at, rows, jobs = 0, {}, []
    for group in groups:
        first = at
        for name, size in group.items():
            rows[name] = (at, size)
            at += size
        at = first + -(-(at - first) // LANES) * LANES
        jobs.append((first, at - first))
    return rows, jobs, at


def kernel(d, *refs):
    s = types.SimpleNamespace(**dict(zip(d.names, refs, strict=True)))
    n, c, ci, r_out, nch = d.images, d.channels, d.inputs, d.rows, d.channels // LANES
    ca = d.augmented
    half = min(256, c)
    halves = c // half
    width = d.width
    h_in = 2 * r_out
    block = r_out * n
    points = r_out * block
    group = n // d.ha
    plane = d.ha * d.wa
    chips = d.img // 2
    ha, wa, img = lax.axis_index("ha"), lax.axis_index("wa"), lax.axis_index("img")
    core, chip = img % 2, img // 2
    here = ha * d.wa + wa
    row0, col0 = ha * h_in, wa * h_in
    along_z = [ha] + [(ha + i) % d.ha for i in range(1, d.ha)]
    along_y = [wa] + [(wa + i) % d.wa for i in range(1, d.wa)]
    along_img = [img] + [(img + i) % d.img for i in range(1, d.img)]
    along_x = [2 * ((chip + i) % chips) + core for i in range(1, chips)]
    plane_peers = [(z, y) for z in along_z for y in along_y][1:]
    partner = (ha, wa, img + 1 - 2 * core)

    at = types.SimpleNamespace(**{name: first for name, (first, _) in d.grad_rows.items()})


    def beside(dr, dc):
        return (along_z[dr % d.ha], along_y[dc % d.wa], img)

    def place(g, total):
        return jnp.where(jnp.logical_or(g < 0, g >= total), FAR, g)

    def mask_at(gr, gc, lanes, value=1.0):
        far = jnp.maximum(place(gr, d.ha * h_in), place(gc, d.wa * h_in))
        return spread_lanes(jnp.where(s.lim[...] > far, value, 0.0).astype(F32), lanes)

    def masks_out(r, value=1.0):
        return [mask_at(row0 + 2 * r, col0 + 2 * j, half, value) for j in range(r_out)]

    def rows(r):
        return pl.ds(pl.multiple_of(r * block, block), block)

    def spot(r, j):
        return pl.ds(pl.multiple_of(r * block + j * n, n), n)

    def lanes(k):
        return slice(k * half, (k + 1) * half)

    def quarter(q):
        return slice(q * LANES, (q + 1) * LANES)

    def part(v, j):
        return v[j * n : (j + 1) * n]

    def vec(i):
        return s.vec[i : i + 1, :]

    pieces = [(j, k) for k in range(halves) for j in range(r_out)]

    def over(folds, images, body, steps=r_out):
        def step(r, carry):
            held = list(carry)

            def add(i, k, v):
                held[i * halves + k] = held[i * halves + k] + fold(v)

            def add_image(i, k, v):
                held[(folds + i) * halves + k] = held[(folds + i) * halves + k] + v

            body(r, add, add_image)
            return tuple(held)

        start = (jnp.zeros((8, half), F32),) * (folds * halves) + (jnp.zeros((n, half), F32),) * (images * halves)
        out = lax.fori_loop(0, steps, step, start)
        return [jnp.concatenate(out[i * halves : (i + 1) * halves], axis=1) for i in range(folds + images)]

    def over_rows(count, body):
        return over(count, 0, lambda r, add, _: body(r, add))

    def each_row(body, steps=r_out, first=0):
        def step(r, carry):
            body(r)
            return carry

        lax.fori_loop(first, steps, step, 0)


    def vector_rows(k):
        return -(-2 * nch // 8) * 8 * (2 if k in wide else 1)

    wide = [k for k, count in enumerate(VECTORS) if count > 2]

    def places_of(k):
        if k in wide:
            return s.slots_wide.at[wide.index(k)], s.across_wide.at[wide.index(k)]
        return s.slots.at[k], s.across.at[k]

    def sum_start(k, parts):
        slots, _ = places_of(k)
        lines = vector_rows(k)
        if lines > len(parts) * nch:
            slots[here] = jnp.zeros((lines, LANES), F32)
        for j, value in enumerate(parts):
            total = jnp.sum(value, axis=0, keepdims=True)
            for i in range(nch):
                line = j * nch + i
                slots[here, line : line + 1, :] = total[:, i * LANES : (i + 1) * LANES]
        mine = slots.at[here]
        for z, y in plane_peers:
            pltpu.make_async_remote_copy(
                src_ref=mine, dst_ref=mine, send_sem=s.sum_sems.at[k, 0], recv_sem=s.sum_sems.at[k, 1],
                device_id=(z, y, img), device_id_type=MESH,
            ).start()

    def sum_wait(k, sem):
        got = places_of(k)[0].at[pl.ds(0, plane - 1)]
        pltpu.make_async_copy(got, got, s.sum_sems.at[k, sem]).wait()

    def sum_wait_across(k, sem):
        got = places_of(k)[1].at[pl.ds(0, d.img - 1)]
        pltpu.make_async_copy(got, got, s.sum_sems.at[k, sem]).wait()

    def sum_finish(k):
        slots, across = places_of(k)
        lines = vector_rows(k)
        sum_wait(k, 1)
        total = slots[0]
        for i in range(1, plane):
            total = total + slots[i]
        across[img] = total
        mine = across.at[img]
        for x in along_img[1:]:
            pltpu.make_async_remote_copy(
                src_ref=mine, dst_ref=mine, send_sem=s.sum_sems.at[k, 2], recv_sem=s.sum_sems.at[k, 3],
                device_id=(ha, wa, x), device_id_type=MESH,
            ).start()
        sum_wait_across(k, 3)
        total = across[0]
        for i in range(1, d.img):
            total = total + across[i]
        s.reduced[0:lines, :] = total
        return [
            jnp.concatenate([s.reduced[j * nch + i : j * nch + i + 1, :] for i in range(nch)], axis=1)
            for j in range(VECTORS[k])
        ]

    def keep(m, i, k=None):
        return s.keep[8 * m + i : 8 * m + i + 1, slice(None) if k is None else lanes(k)]

    def set_norm(m, total, square, inverse, gain, shift):
        center = total * inverse
        factor = lax.rsqrt(square * inverse - center * center + EPS)
        scale = factor * vec(gain)
        offset = vec(shift) - center * scale
        for i, value in enumerate((center, factor, 0.5 * scale, 0.5 * offset, scale)):
            s.keep[8 * m + i : 8 * m + i + 1, :] = value

    def set_back(m, shift_sum, weighted, inverse, out, raised=0.0):
        center, factor, scale = keep(m, 0), keep(m, 1), keep(m, 4)
        gain_sum = (weighted - (center + raised) * shift_sum) * factor
        slope = -(scale * factor * gain_sum * inverse)
        offset = -(scale * shift_sum * inverse) - slope * center
        for i, value in enumerate((scale, slope, offset)):
            s.keep[8 * m + 5 + i : 8 * m + 6 + i, :] = value
        s.vectors[out : out + 1, :] = gain_sum
        s.vectors[out + 1 : out + 2, :] = shift_sum

    def back(m, upstream, field, mask, k):
        return (upstream * keep(m, 5, k) + (field * keep(m, 6, k) + keep(m, 7, k)) * mask).astype(BF16)


    def tiles_start(e, terms):
        s.tile_slots[e, here, :, 0 : terms.shape[1]] = terms.astype(BF16)
        mine = s.tile_slots.at[e, here]
        for z, y in plane_peers:
            pltpu.make_async_remote_copy(
                src_ref=mine, dst_ref=mine, send_sem=s.tile_sems.at[e, 0], recv_sem=s.tile_sems.at[e, 1],
                device_id=(z, y, img), device_id_type=MESH,
            ).start()

    def tiles_wait(e, sem):
        got = s.tile_slots.at[e, pl.ds(0, plane - 1)]
        pltpu.make_async_copy(got, got, s.tile_sems.at[e, sem]).wait()

    def tiles_finish(e, units):
        tiles_wait(e, 1)
        total = s.tile_slots[e, 0].astype(F32)
        for i in range(1, plane):
            total = total + s.tile_slots[e, i].astype(F32)
        return total[:, 0:units]

    def gates_load(parts):
        for i, value in enumerate(parts):
            s.gate_src[:, i] = value.astype(BF16).reshape(d.ha, group, c)

    def gates_start(which):
        s.gate_slots[here] = s.gate_src[ha]
        for z, y in plane_peers:
            pltpu.make_async_remote_copy(
                src_ref=s.gate_src.at[z], dst_ref=s.gate_slots.at[here], send_sem=s.gate_sems.at[which, 0],
                recv_sem=s.gate_sems.at[which, 1], device_id=(z, y, img), device_id_type=MESH,
            ).start()

    def gates_finish(which):
        got = s.gate_slots.at[pl.ds(0, plane - 1)]
        pltpu.make_async_copy(got, got, s.gate_sems.at[which, 1]).wait()
        for i in range(2):
            total = s.gate_slots[0, i].astype(F32)
            for j in range(1, plane):
                total = total + s.gate_slots[j, i].astype(F32)
            s.gates[which, ha, i] = total
        pltpu.make_async_copy(got, got, s.gate_sems.at[which, 0]).wait()
        mine = s.gates.at[which, ha]
        for z in along_z[1:]:
            pltpu.make_async_remote_copy(
                src_ref=mine, dst_ref=mine, send_sem=s.gate_sems.at[which, 2], recv_sem=s.gate_sems.at[which, 3],
                device_id=(z, wa, img), device_id_type=MESH,
            ).start()

    def gates_wait(which, sem):
        got = s.gates.at[which, pl.ds(0, d.ha - 1)]
        pltpu.make_async_copy(got, got, s.gate_sems.at[which, sem]).wait()

    def img_wait(which, sem):
        got = s.group_x.at[which, pl.ds(0, d.img - 1)]
        pltpu.make_async_copy(got, got, s.group_sems.at[which, sem]).wait()

    def img_start(which, rows_):
        for j, row in enumerate(rows_):
            for i in range(nch):
                line = j * nch + i
                s.group_x[which, img, line : line + 1, :] = row[:, i * LANES : (i + 1) * LANES]
        mine = s.group_x.at[which, img]
        for x in along_img[1:]:
            pltpu.make_async_remote_copy(
                src_ref=mine, dst_ref=mine, send_sem=s.group_sems.at[which, 0], recv_sem=s.group_sems.at[which, 1],
                device_id=(ha, wa, x), device_id_type=MESH,
            ).start()

    def img_finish(which):
        img_wait(which, 1)
        total = s.group_x[which, 0]
        for i in range(1, d.img):
            total = total + s.group_x[which, i]
        s.reduced[0 : 2 * nch, :] = total[0 : 2 * nch]
        return [
            jnp.concatenate([s.reduced[j * nch + i : j * nch + i + 1, :] for i in range(nch)], axis=1)
            for j in range(2)
        ]

    def every(j, k):
        return s.shared[j, :, :, lanes(k)].reshape(n, half)

    def inverse_pixels():
        return spread_lanes(s.invpix[...].reshape(n, LANES), c)

    def excite_forward(j, excitation, sums):
        e = excitation
        pooled = sums * inverse_pixels()
        tiles_start(j, fine(mt if e.turned else mm, pooled, e.down[...]))
        e.pooled[...] = pooled
        before = tiles_finish(j, e.units) + vec(e.down_bias)[:, : e.units]
        e.before[...] = before
        scaling = sigmoid(fine(mm, before * sigmoid(before), e.up[...]) + vec(e.up_bias))
        s.shared[j] = scaling.reshape(d.ha, group, c)

    def excite_backward_start(j, forward, excitation, sums):
        scaling = s.shared[forward].reshape(n, c)
        dlogit = sums * scaling * (1.0 - scaling)
        tiles_start(j, fine(mt, dlogit, excitation.up[...]))
        s.dlogit[...] = dlogit

    def excite_backward(j, excitation, which):
        e = excitation
        before = e.before[...]
        logistic = sigmoid(before)
        dbefore = tiles_finish(j, e.units) * (logistic * (1.0 + before * (1.0 - logistic)))
        dpooled = fine(mm if e.turned else mt, dbefore, e.down[...]) * inverse_pixels()
        img_start(
            which,
            [jnp.sum(dpooled * s.gates[which, :, i].reshape(n, c), axis=0, keepdims=True) for i in range(2)],
        )
        s.shared[j] = dpooled.reshape(d.ha, group, c)
        dlogit = s.dlogit[...]
        s.stage[e.up_at : e.up_at + e.units, :] = exact_tm(before * logistic, dlogit).astype(BF16)
        if e.turned:
            s.stage[e.down_at : e.down_at + e.units, :] = exact_tm(dbefore, e.pooled[...]).astype(BF16)
        else:
            down = exact_tm(e.pooled[...], dbefore)
            for i in range(nch):
                s.stage[e.down_at : e.down_at + LANES, quarter(i)] = down[quarter(i)].astype(BF16)
        owner = jnp.where(here == 0, 1.0, 0.0).astype(F32)
        s.biases[e.bias_at : e.bias_at + 1, :] = jnp.sum(dlogit, axis=0, keepdims=True)
        s.biases[e.bias_at + 1 : e.bias_at + 2, 0 : e.units] = jnp.sum(dbefore, axis=0, keepdims=True) * owner

    one = types.SimpleNamespace(
        turned=True, down=s.squeeze, up=s.excite, units=d.hidden_one, down_bias=SQUEEZE_B, up_bias=EXCITE_B,
        pooled=s.pooled_one, before=s.before_one, down_at=at.squeeze, up_at=at.excite, bias_at=0,
    )
    two = types.SimpleNamespace(
        turned=False, down=s.reduce, up=s.expand, units=d.hidden_two, down_bias=REDUCE_B, up_bias=EXPAND_B,
        pooled=s.pooled_two, before=s.before_two, down_at=at.reduce, up_at=at.expand, bias_at=2,
    )


    class Reduction:
        def __init__(self, index):
            self.index = index
            self.first, self.size = d.jobs[index]
            self.direct = index == 3
            self.hr = self.size if self.direct else self.size // 2
            self.pr = self.hr // d.ha
            self.slot = pl.ds(self.first // (2 * d.ha), self.pr)
            self.mine = self.first if self.direct else self.first + core * self.hr
            self.other = self.first + (1 - core) * self.hr
            self.apart = index >= 2
            self.home = s.excited_two if self.apart else s.stage
            self.shift = d.jobs[2][0] if self.apart else 0

        def sem(self, i):
            return s.grad_sems.at[self.index, i]

        def half_at(self, ref, first):
            return ref.at[pl.ds(pl.multiple_of(first, 16), self.hr)]

        def piece(self, ref, z, y, shift=0):
            first = pl.multiple_of(self.mine - shift + z * self.pr, 16)
            return ref.at[pl.ds(first, self.pr), pl.ds(pl.multiple_of(y * LANES, LANES), LANES)]

        def wait(self, ref, sem):
            pltpu.make_async_copy(ref, ref, self.sem(sem)).wait()

        def swapped(self):
            return s.swaps.at[pl.ds(self.first // 2, self.hr)]

        def many(self):
            return s.scattered.at[pl.ds(0, plane - 1), self.slot]

        def swap(self):
            pltpu.make_async_remote_copy(
                src_ref=self.half_at(s.stage, self.other), dst_ref=self.swapped(), send_sem=self.sem(0),
                recv_sem=self.sem(1), device_id=partner, device_id_type=MESH,
            ).start()

        def scatter(self):
            lines = min(32, self.pr)

            def add(i):
                mine = pl.ds(pl.multiple_of(self.mine + i * lines, 16), lines)
                theirs = pl.ds(pl.multiple_of(self.first // 2 + i * lines, 16), lines)
                s.stage[mine, :] = (s.stage[mine, :].astype(F32) + s.swaps[theirs, :].astype(F32)).astype(BF16)

            if not self.direct:
                self.wait(self.swapped(), 1)
                each_row(add, self.hr // lines)
            for z, y in plane_peers:
                pltpu.make_async_remote_copy(
                    src_ref=self.piece(s.stage, z, y), dst_ref=s.scattered.at[here, self.slot],
                    send_sem=self.sem(2), recv_sem=self.sem(3), device_id=(z, y, img), device_id_type=MESH,
                ).start()
            s.scattered[here, self.slot] = self.piece(s.stage, ha, wa)[...]

        def level(self):
            if self.direct:
                return s.crossed_all, img, d.img, pl.ds(0, self.pr), along_img[1:]
            return s.crossed, chip, chips, self.slot, along_x

        def exchange(self):
            self.wait(self.many(), 3)
            places, own, _, slot, peers = self.level()

            def add(i):
                lines = pl.ds(pl.multiple_of(self.slot.start + i * 16, 16), 16)
                total = s.scattered[0, lines].astype(F32)
                for j in range(1, plane):
                    total = total + s.scattered[j, lines].astype(F32)
                places[own, pl.ds(pl.multiple_of(slot.start + i * 16, 16), 16)] = total.astype(BF16)

            each_row(add, self.pr // 16)
            mine = places.at[own, slot]
            for x in peers:
                pltpu.make_async_remote_copy(
                    src_ref=mine, dst_ref=mine, send_sem=self.sem(4), recv_sem=self.sem(5),
                    device_id=(ha, wa, x), device_id_type=MESH,
                ).start()

        def wait_crossing(self, sem):
            places, _, count, slot, _ = self.level()
            if count > 1:
                self.wait(places.at[pl.ds(0, count - 1), slot], sem)

        def gather(self):
            self.wait_crossing(5)
            places, _, count, slot, _ = self.level()

            def add(i):
                lines = pl.ds(pl.multiple_of(slot.start + i * 16, 16), 16)
                total = places[0, lines].astype(F32)
                for j in range(1, count):
                    total = total + places[j, lines].astype(F32)
                s.summed[pl.ds(pl.multiple_of(self.slot.start + i * 16, 16), 16)] = total.astype(BF16)

            each_row(add, self.pr // 16)
            mine = self.piece(self.home, ha, wa, self.shift)
            mine[...] = s.summed[self.slot]
            for z, y in plane_peers:
                pltpu.make_async_remote_copy(
                    src_ref=s.summed.at[self.slot], dst_ref=mine, send_sem=self.sem(6), recv_sem=self.sem(7),
                    device_id=(z, y, img), device_id_type=MESH,
                ).start()

        def hand(self):
            self.wait(self.many(), 7)
            if self.direct:
                return
            mine = self.half_at(self.home, self.mine - self.shift)
            pltpu.make_async_remote_copy(
                src_ref=mine, dst_ref=mine, send_sem=self.sem(8), recv_sem=self.sem(9),
                device_id=partner, device_id_type=MESH,
            ).start()

        def finish(self):
            if not self.direct:
                self.wait(self.half_at(self.home, self.other - self.shift), 9)
                self.wait(self.half_at(self.home, self.mine - self.shift), 8)
            self.wait(self.many(), 6)
            self.wait_crossing(4)
            if self.apart:
                self.settle()
                lines = min(32, self.size)

                def bring(i):
                    there = pl.ds(pl.multiple_of(self.first + i * lines, 16), lines)
                    here_ = pl.ds(pl.multiple_of(self.first - self.shift + i * lines, 16), lines)
                    s.stage[there, :] = s.excited_two[here_, :]

                each_row(bring, self.size // lines)

        def settle(self):
            self.wait(self.many(), 2)
            if not self.direct:
                self.wait(self.half_at(s.stage, self.other), 0)

    jobs = [Reduction(i) for i in range(len(d.jobs))]


    around = [(dr, dc) for dr in (-1, 0, 1) for dc in (-1, 0, 1) if (dr, dc) != (0, 0)]

    def edge(step):
        if step == 0:
            return pl.ds(1, r_out), pl.ds(1, r_out)
        return (pl.ds(r_out, 1), pl.ds(0, 1)) if step > 0 else (pl.ds(1, 1), pl.ds(r_out + 1, 1))

    def ring_copies(frame, h):
        copies = []
        for i, (dr, dc) in enumerate(around):
            (from_r, to_r), (from_c, to_c) = edge(dr), edge(dc)
            copies.append(
                pltpu.make_async_remote_copy(
                    src_ref=frame.at[from_r, from_c], dst_ref=frame.at[to_r, to_c],
                    send_sem=s.ring_send.at[h, i], recv_sem=s.ring_recv.at[h, i],
                    device_id=beside(dr, dc), device_id_type=MESH,
                )
            )
        return copies

    def three_copies(parts, send, recv):
        return [
            pltpu.make_async_remote_copy(
                src_ref=src, dst_ref=dst, send_sem=send.at[i], recv_sem=recv.at[i],
                device_id=beside(*to), device_id_type=MESH,
            )
            for i, (src, dst, to) in enumerate(parts)
        ]

    def rim_copies():
        last = h_in - 1
        parts = (
            (s.images.at[last], s.rim.at[0], (1, 0)),
            (s.images.at[pl.ds(0, h_in), last], s.rim.at[1], (0, 1)),
            (s.images.at[last, pl.ds(last, 1)], s.rim_corner, (1, 1)),
        )
        return three_copies(parts, s.rim_send, s.rim_recv)

    def corner_copies(frame):
        first, all_, last = pl.ds(0, 1), pl.ds(0, r_out), pl.ds(r_out, 1)
        parts = (
            (frame.at[first, all_], frame.at[last, all_], (-1, 0)),
            (frame.at[all_, first], frame.at[all_, last], (0, -1)),
            (frame.at[first, first], frame.at[last, last], (-1, -1)),
        )
        return three_copies(parts, s.corner_send, s.corner_recv)


    def same_group():
        down = lax.broadcasted_iota(jnp.int32, (half, half), 0) // width
        across = lax.broadcasted_iota(jnp.int32, (half, half), 1) // width
        return jnp.where(down == across, 1.0, 0.0).astype(F32)

    def block_diagonal(source, t, k, same):
        return jnp.concatenate([source[t, :, lanes(k)]] * (half // width), axis=0) * same

    def build_kernel(source):
        same = same_group().astype(BF16)

        def tap(t):
            for k in range(halves):
                s.taps[k, pl.ds(pl.multiple_of(t * half, half), half), :] = block_diagonal(source, t, k, same)

        each_row(tap, 9)

    def build_turned(source, order):
        same = same_group().astype(BF16)
        for i, t in enumerate(order):
            for k in range(halves):
                s.taps[k, i * half : (i + 1) * half, :] = block_diagonal(source, t, k, same).T

    def kernel_grad(dz, window, first):
        down = lax.broadcasted_iota(jnp.int32, (LANES, LANES), 0) // width
        across = lax.broadcasted_iota(jnp.int32, (LANES, LANES), 1) // width
        same = jnp.where(down == across, 1.0, 0.0).astype(F32)
        for q in range(nch):
            s.turned[q] = dz(q).T

        def pair(t):
            taps = [2 * t, jnp.minimum(2 * t + 1, 8)]
            for q in range(nch):
                windows = [window(tap // 3, tap % 3, q) for tap in taps]
                got = mm(s.turned[q], jnp.concatenate(windows, axis=1)).T
                for i, tap in enumerate(taps):
                    block_ = got[i * LANES : (i + 1) * LANES] * same
                    total = block_[0:width]
                    for g in range(1, LANES // width):
                        total = total + block_[g * width : (g + 1) * width]
                    there = pl.ds(pl.multiple_of(first + tap * width, 16), width)
                    s.stage[there, quarter(q)] = total.astype(BF16)

        each_row(pair, 5)

    def product_grad(left, columns, first):
        def some(j):
            span = pl.ds(pl.multiple_of(j * LANES, LANES), LANES)
            got = tm(left(span), s.cot[...].reshape(points, c))
            s.stage[pl.ds(pl.multiple_of(first + j * LANES, 16), LANES), :] = got.astype(BF16)

        each_row(some, columns // LANES)

    def strided(i, ph, pw):
        return jnp.concatenate([s.x[2 * i + ph, 2 * j + pw] for j in range(r_out)], axis=0)

    def bypass(sources, k):
        return mm(sources, s.short_rows[:, lanes(k)])

    def augment(raw, gr, gc):
        mask = mask_at(gr, gc, LANES)
        lane = lax.broadcasted_iota(jnp.int32, (n, ca - ci), 1)
        more = jnp.where(lane < 3, mask[:, : ca - ci], 0.0)
        return jnp.concatenate([raw.astype(F32) * spread_lanes(mask, ci), more], axis=1).astype(BF16)

    def below(value_rows):
        row = lax.broadcasted_iota(jnp.int32, (ca - ci, c), 0)
        total = jnp.zeros((ca - ci, c), F32)
        for i, value in enumerate(value_rows):
            total = jnp.where(row == i, value.astype(F32), total)
        return total

    def gram_moments(gram, kernel_rows):
        parts = in_parts(gram[0:ci, 0:ci], 3)
        product = sum(mm(p, kernel_rows[...]) for p in parts)
        square = jnp.sum(product * kernel_rows[...].astype(F32), axis=0, keepdims=True)
        total = sum(mm(p, kernel_rows[...]) for p in in_parts(gram[ci : ci + 16, 0:ci], 3))[0:1]
        return total, square

    def residual_row(r):
        return s.residual[r + 1, pl.ds(1, r_out)].reshape(block, c)

    def augment(raw, gr, gc):
        mask = mask_at(gr, gc, LANES)
        lane = lax.broadcasted_iota(jnp.int32, (n, ca - ci), 1)
        more = jnp.where(lane < 3, mask[:, : ca - ci], 0.0)
        return jnp.concatenate([raw.astype(F32) * spread_lanes(mask, ci), more], axis=1).astype(BF16)

    def below(value_rows):
        row = lax.broadcasted_iota(jnp.int32, (ca - ci, c), 0)
        total = jnp.zeros((ca - ci, c), F32)
        for i, value in enumerate(value_rows):
            total = jnp.where(row == i, value.astype(F32), total)
        return total

    def gram_moments(gram, kernel_rows):
        parts = in_parts(gram[0:ci, 0:ci], 3)
        product = sum(mm(p, kernel_rows[...]) for p in parts)
        square = jnp.sum(product * kernel_rows[...].astype(F32), axis=0, keepdims=True)
        total = sum(mm(p, kernel_rows[...]) for p in in_parts(gram[ci : ci + 16, 0:ci], 3))[0:1]
        return total, square

    def residual_row(r):
        return s.residual[r + 1, pl.ds(1, r_out)].reshape(block, c)

    def second(r, k):
        return mm(residual_row(r), s.second_kernel[:, lanes(k)])


    depth = s.raw.shape[0]

    def load(h):
        return pltpu.make_async_copy(s.images.at[h], s.raw.at[h % depth], s.load_sems.at[h % depth])

    for h in range(depth):
        load(h).start()
    cot_load = pltpu.make_async_copy(s.cotangent, s.cot, s.cot_sem.at[0])
    cot_load.start()
    weight_loads = [
        pltpu.make_async_copy(getattr(s, name + SENT), getattr(s, name), s.weight_sems.at[i])
        for i, name in enumerate(d.weights)
    ]
    for copy in weight_loads:
        copy.start()
    vec_loads = [
        pltpu.make_async_copy(getattr(s, name), s.vec.at[i, pl.ds(0, size)], s.vec_sems.at[i])
        for i, (name, size) in enumerate(d.vectors)
    ]
    for copy in vec_loads:
        copy.start()

    barrier = pltpu.get_barrier_semaphore()
    for z, y in plane_peers:
        pl.semaphore_signal(barrier, inc=1, device_id=(z, y, img), device_id_type=MESH)
    for x in along_img[1:]:
        pl.semaphore_signal(barrier, inc=1, device_id=(ha, wa, x), device_id_type=MESH)

    classes = s.classes[...]
    slot = lax.broadcasted_iota(jnp.int32, classes.shape, 1)
    side = 10 + 4 * classes
    index = lax.broadcasted_iota(jnp.int32, classes.shape, 0)
    counts = jnp.zeros(classes.shape, jnp.int32)
    for i in range(d.img):
        counts = jnp.where(index == i, s.image_counts[i], counts)
    cells = jnp.sum(jnp.where(slot < counts, (side * side).astype(F32), 0.0), axis=1, keepdims=True)
    inv_out = 1.0 / jnp.sum(cells, axis=0, keepdims=True)
    inv_in = 0.25 * inv_out
    own_side = (10 + 4 * s.classes[pl.ds(img, 1), :]).astype(F32)
    spread = jnp.broadcast_to(own_side, (n, n))
    diagonal = lax.broadcasted_iota(jnp.int32, (n, n), 0) == lax.broadcasted_iota(jnp.int32, (n, n), 1)
    sides = jnp.sum(jnp.where(diagonal, spread, 0.0), axis=1, keepdims=True)
    sides = jnp.broadcast_to(sides, (n, LANES))
    alive = lax.broadcasted_iota(jnp.int32, (n, LANES), 0) < s.image_counts[img]
    s.lim[...] = jnp.where(alive, 2.0 * sides, 0.0).astype(jnp.int32)
    s.invpix[...] = (1.0 / (sides * sides)).reshape(d.ha, group, LANES)
    s.biases[...] = jnp.zeros((16, c), F32)

    s.gram[...] = jnp.zeros((ca, ca), F32)
    s.gathered[:, 0:ca] = jnp.zeros((ca, ca), F32)

    def load_rows(i):
        for h in (2 * i, 2 * i + 1):
            load(h).wait()
            for w in range(h_in):
                s.x[h, w] = augment(s.raw[h % depth, w], row0 + h, col0 + w)

            @pl.when(h + depth < h_in)
            def _(h=h):
                load(h + depth).start()

            x = s.x[h].reshape(h_in * n, ca)
            s.gram[...] += tm(x, x)
        x = strided(i, 0, 0)
        s.gathered[:, 0:ca] += tm(x, x)

    each_row(load_rows, 2)
    pl.semaphore_wait(barrier, plane - 1 + d.img - 1)
    rims = rim_copies()
    for copy in rims:
        copy.start()
    each_row(load_rows, r_out, 2)
    sums_a = gram_moments(s.gram, s.entry_kernel)
    sum_start(SUM_A, sums_a + gram_moments(s.gathered, s.shortcut_kernel))
    for copy in weight_loads:
        copy.wait()
    build_kernel(s.group_kernel)
    s.entry_rows[0:ci, :] = s.entry_kernel[...]
    s.short_rows[0:ci, :] = s.shortcut_kernel[...]
    s.short_rows[ci:ca, :] = jnp.zeros((ca - ci, c), BF16)
    for copy in vec_loads:
        copy.wait()
    total_a, square_a, total_s, square_s = sum_finish(SUM_A)
    set_norm(A_, total_a, square_a, inv_in, ENTRY_G, ENTRY_S)
    set_norm(S_, total_s, square_s, inv_out, SHORT_G, SHORT_S)
    raised = vec(ENTRY_S) / keep(A_, 4) - keep(A_, 0)
    s.entry_rows[ci:ca, :] = below(in_parts(raised, 3)).astype(BF16)

    def activate(x, count, store):
        for k in range(halves):
            entry = mm(x, s.entry_rows[:, lanes(k)])
            for j in range(count):
                store(j, k, silu_half(part(entry, j) * keep(A_, 2, k)).astype(BF16))

    def active_row(h):
        for q in range(2):
            def store(j, k, value, q=q):
                s.active[h + 1, 1 + r_out * q + j, :, lanes(k)] = value

            activate(s.x[h, pl.ds(r_out * q, r_out)].reshape(block, ca), r_out, store)

    each_row(active_row, h_in)
    for copy in rims:
        copy.wait_recv()

    for q in range(2):
        def store_top(j, k, value, q=q):
            s.active[0, 1 + r_out * q + j, :, lanes(k)] = value

        def store_left(j, k, value, q=q):
            s.active[1 + r_out * q + j, 0, :, lanes(k)] = value

        for j in range(r_out):
            s.rim_rows[j] = augment(s.rim[0, r_out * q + j], row0 - 1, col0 + r_out * q + j)
        activate(s.rim_rows[...].reshape(block, ca), r_out, store_top)
        for j in range(r_out):
            s.rim_rows[j] = augment(s.rim[1, r_out * q + j], row0 + r_out * q + j, col0 - 1)
        activate(s.rim_rows[...].reshape(block, ca), r_out, store_left)

    def store_corner(j, k, value):
        s.active[0, 0, :, lanes(k)] = value

    activate(augment(s.rim_corner[0], row0 - 1, col0 - 1), 1, store_corner)


    def convolve(window, store):
        def row(r, add):
            masks = masks_out(r)
            for k in range(halves):
                windows = [window(r, ky, kx, k) for ky in range(3) for kx in range(3)]
                field = mm(jnp.concatenate(windows, axis=1), s.taps[k])
                store[rows(r), lanes(k)] = field.astype(BF16)
                for j in range(r_out):
                    masked = part(field, j) * masks[j]
                    add(0, k, masked)
                    add(1, k, masked * part(field, j))

        return over_rows(2, row)

    def window_one(r, ky, kx, k):
        return jnp.concatenate([s.active[2 * r + ky, 2 * j + kx, :, lanes(k)] for j in range(r_out)], axis=0)

    sum_start(SUM_B, convolve(window_one, s.middle))
    build_kernel(s.spatial_kernel)
    set_norm(B_, *sum_finish(SUM_B), inv_out, GROUP_G, GROUP_S)

    def gated(m, store, r, j, k, mask):
        return silu_half(store[spot(r, j), lanes(k)].astype(F32) * keep(m, 2, k) + keep(m, 3, k)) * mask

    def gated_sums(m, store):
        def row(r, add, add_image):
            masks = masks_out(r)
            for j, k in pieces:
                add_image(0, k, gated(m, store, r, j, k, masks[j]))

        return over(0, 1, row)[0]

    def slope_sums(m, store):
        def row(r, add, add_image):
            masks_half = masks_out(r, 0.5)
            for j, k in pieces:
                field = store[spot(r, j), lanes(k)].astype(F32)
                _, slope = silu_and_slope(field * keep(m, 2, k) + keep(m, 3, k))
                slope = slope * masks_half[j]
                add_image(0, k, slope)
                add_image(1, k, slope * field)

        return over(0, 2, row)

    def excite_row(r, m, store, forward, excited):
        masks = masks_out(r)
        for j, k in pieces:
            value = gated(m, store, r, j, k, masks[j]) * every(forward, k)
            excited[spot(r, j), lanes(k)] = value.astype(BF16)

    excite_forward(0, one, gated_sums(B_, s.middle))

    def branch_row(r, add):
        excite_row(r, B_, s.middle, 0, s.excited_one)
        for k in range(halves):
            field = mm(s.excited_one[rows(r), :], s.output_kernel[:, lanes(k)])
            s.branch[rows(r), lanes(k)] = field.astype(BF16)
            add(0, k, field)
            add(1, k, field * field)

    sum_start(SUM_C, over_rows(2, branch_row))
    gates_load(slope_sums(B_, s.middle))
    set_norm(C_, *sum_finish(SUM_C), inv_out, OUTPUT_G, OUTPUT_S)


    def total_one_half(field, skip, k):
        return field * keep(C_, 2, k) + skip * keep(S_, 2, k) + (keep(C_, 3, k) + keep(S_, 3, k))

    def second_row(r, add):
        masks, sources = masks_out(r), strided(r, 0, 0)
        for k in range(halves):
            skip = bypass(sources, k)
            for j in range(r_out):
                field = s.branch[spot(r, j), lanes(k)].astype(F32)
                value = silu_half(total_one_half(field, part(skip, j), k)) * masks[j]
                s.residual[r + 1, 1 + j, :, lanes(k)] = value.astype(BF16)
        for k in range(halves):
            field = mm(residual_row(r), s.second_kernel[:, lanes(k)])
            s.second[rows(r), lanes(k)] = field.astype(BF16)
            add(0, k, field)
            add(1, k, field * field)

    sums_d = over_rows(2, second_row)
    ring = ring_copies(s.residual, 0)
    for copy in ring:
        copy.start()
    sum_start(SUM_D, sums_d)
    s.square_t[...] = s.final_kernel[...].T
    set_norm(D_, *sum_finish(SUM_D), inv_out, SECOND_G, SECOND_S)
    gates_start(0)

    def put_active_two(field, fr, fc, k):
        mask = mask_at(row0 + 2 * (fr - 1), col0 + 2 * (fc - 1), half)
        value = silu_half(field * keep(D_, 2, k) + keep(D_, 3, k)) * mask
        s.frame[fr, fc, :, lanes(k)] = value.astype(BF16)

    def active_two(x, places):
        for k in range(halves):
            field = mm(x, s.second_kernel[:, lanes(k)])
            for j, (fr, fc) in enumerate(places):
                put_active_two(part(field, j), fr, fc, k)

    def active_two_row(r):
        for j, k in pieces:
            put_active_two(s.second[spot(r, j), lanes(k)].astype(F32), r + 1, 1 + j, k)

    each_row(active_two_row)
    for copy in ring:
        copy.wait_recv()
    for fr in (0, r_out + 1):
        x = s.residual[fr].reshape((r_out + 2) * n, c)
        active_two(x, [(fr, fc) for fc in range(r_out + 2)])
    for fc in (0, r_out + 1):
        x = s.residual[pl.ds(1, r_out), fc].reshape(block, c)
        active_two(x, [(fr, fc) for fr in range(1, r_out + 1)])

    def window_two(r, ky, kx, k):
        return s.frame[r + ky, pl.ds(kx, r_out), :, lanes(k)].reshape(block, half)

    sum_start(SUM_E, convolve(window_two, s.spatial))
    s.start_rows[0:c, :] = s.shortcut_kernel[...].T
    gates_finish(0)
    set_norm(E_, *sum_finish(SUM_E), inv_out, SPATIAL_G, SPATIAL_S)

    excite_forward(1, two, gated_sums(E_, s.spatial))

    def final_row(r, add):
        excite_row(r, E_, s.spatial, 1, s.excited_two)
        for k in range(halves):
            field = mm(s.excited_two[rows(r), :], s.final_kernel[:, lanes(k)])
            s.field[rows(r), lanes(k)] = field
            add(0, k, field)
            add(1, k, field * field)

    sum_start(SUM_F, over_rows(2, final_row))
    cot_load.wait()
    build_turned(s.spatial_kernel, range(9))
    gates_load(slope_sums(E_, s.spatial))
    set_norm(F_, *sum_finish(SUM_F), inv_out, FINAL_G, FINAL_S)
    gates_start(1)


    def top_row(r, add):
        masks, masks_half = masks_out(r), masks_out(r, 0.5)
        for j, k in pieces:
            field = s.field[spot(r, j), lanes(k)]
            kept = s.residual[r + 1, 1 + j, :, lanes(k)].astype(F32)
            value, slope = silu_and_slope(field * keep(F_, 2, k) + keep(F_, 3, k) + 0.5 * kept)
            upstream = s.cot[r, j, :, lanes(k)].astype(F32) * masks_half[j] * slope
            s.cot[r, j, :, lanes(k)] = (value * masks[j]).astype(BF16)
            s.upstream[spot(r, j), lanes(k)] = upstream
            add(0, k, upstream)
            add(1, k, upstream * field)

    sum_start(BACK_F, over_rows(2, top_row))
    gates_finish(1)
    activations_out = pltpu.make_async_copy(s.cot, s.activations, s.cot_sem.at[1])
    activations_out.start()
    set_back(F_, *sum_finish(BACK_F), inv_out, FINAL_G)
    activations_out.wait()

    def excited_back(r, add, add_image, m, store, forward):
        masks, masks_half = masks_out(r), masks_out(r, 0.5)
        dz = s.cot[r].reshape(block, c)
        for k in range(halves):
            dexcited = mm(dz, s.square_t[:, lanes(k)])
            s.field[rows(r), lanes(k)] = dexcited
            for j in range(r_out):
                field = store[spot(r, j), lanes(k)].astype(F32)
                value, slope = silu_and_slope(field * keep(m, 2, k) + keep(m, 3, k))
                add_image(0, k, part(dexcited, j) * (value * masks[j]))
                upstream = part(dexcited, j) * every(forward, k) * (slope * masks_half[j])
                add(0, k, upstream)
                add(1, k, upstream * field)

    def final_back(r, add, add_image):
        masks = masks_out(r)
        for j, k in pieces:
            upstream, field = s.upstream[spot(r, j), lanes(k)], s.field[spot(r, j), lanes(k)]
            s.cot[r, j, :, lanes(k)] = back(F_, upstream, field, masks[j], k)
        excited_back(r, add, add_image, E_, s.spatial, 1)

    *sums_e, dscaling_sums = over(2, 1, final_back)
    excite_backward_start(2, 1, two, dscaling_sums)
    sum_start(BACK_E, sums_e)
    product_grad(lambda span: s.excited_two[0:points, span], c, at.final)
    gates_wait(1, 3)
    excite_backward(2, two, 1)

    def gate_back(m, forward, backward, store, put):
        def row(r):
            masks, masks_half = masks_out(r), masks_out(r, 0.5)
            for j, k in pieces:
                field = store[spot(r, j), lanes(k)].astype(F32)
                _, slope = silu_and_slope(field * keep(m, 2, k) + keep(m, 3, k))
                dgated = s.field[spot(r, j), lanes(k)] * every(forward, k) + every(backward, k)
                put(r, j, k, back(m, dgated * masks_half[j] * slope, field, masks[j], k))

        each_row(row)

    def finish_gate(k, which):
        shift_sum, weighted = sum_finish(k)
        more_shift, more_weighted = img_finish(which)
        return shift_sum + more_shift, weighted + more_weighted

    set_back(E_, *finish_gate(BACK_E, 1), inv_out, SPATIAL_G)

    def put_spatial(r, j, k, dz):
        s.dframe[r + 1, 1 + j, :, lanes(k)] = dz

    gate_back(E_, 1, 2, s.spatial, put_spatial)
    ring_back = ring_copies(s.dframe, 1)
    for copy in ring_back:
        copy.start()
    inner = pl.ds(1, r_out)
    outer = pl.ds(0, r_out)

    def all_two(ky, kx, q):
        return s.frame[pl.ds(ky, r_out), pl.ds(kx, r_out), :, quarter(q)].reshape(points, LANES)

    kernel_grad(lambda q: s.dframe[inner, inner, :, quarter(q)].reshape(points, LANES), all_two, at.spatial)
    for copy in ring_back:
        copy.wait_recv()
    blank = jnp.zeros((r_out + 2, n, c), BF16)

    @pl.when(ha == 0)
    def _():
        s.dframe[0] = blank

    @pl.when(ha == d.ha - 1)
    def _():
        s.dframe[r_out + 1] = blank

    @pl.when(wa == 0)
    def _():
        s.dframe[:, 0] = blank

    @pl.when(wa == d.wa - 1)
    def _():
        s.dframe[:, r_out + 1] = blank

    def second_back(r, add):
        masks = masks_out(r, 0.5)
        for k in range(halves):
            windows = [
                s.dframe[r + 2 - ky, pl.ds(2 - kx, r_out), :, lanes(k)].reshape(block, half)
                for ky in range(3)
                for kx in range(3)
            ]
            total = mm(jnp.concatenate(windows, axis=1), s.taps[k])
            for j in range(r_out):
                field = s.second[spot(r, j), lanes(k)].astype(F32)
                _, slope = silu_and_slope(field * keep(D_, 2, k) + keep(D_, 3, k))
                upstream = part(total, j) * masks[j] * slope
                s.field[spot(r, j), lanes(k)] = upstream
                add(0, k, upstream)
                add(1, k, upstream * field)

    sum_start(BACK_D, over_rows(2, second_back))
    jobs[0].swap()
    build_turned(s.group_kernel, PARITY_TAPS)
    s.square_t[...] = s.second_kernel[...].T
    set_back(D_, *sum_finish(BACK_D), inv_out, SECOND_G)


    def residual_back(r, add):
        masks, masks_half, sources = masks_out(r), masks_out(r, 0.5), strided(r, 0, 0)
        for j, k in pieces:
            upstream, field = s.field[spot(r, j), lanes(k)], s.second[spot(r, j), lanes(k)].astype(F32)
            s.cot[r, j, :, lanes(k)] = back(D_, upstream, field, masks[j], k)
        dz = s.cot[r].reshape(block, c)
        for k in range(halves):
            dresidual, skips = mm(dz, s.square_t[:, lanes(k)]), bypass(sources, k)
            for j in range(r_out):
                field, skip = s.branch[spot(r, j), lanes(k)].astype(F32), part(skips, j)
                _, slope = silu_and_slope(total_one_half(field, skip, k))
                upstream = (s.upstream[spot(r, j), lanes(k)] + part(dresidual, j)) * masks_half[j] * slope
                s.field[spot(r, j), lanes(k)] = upstream
                add(0, k, upstream)
                add(1, k, upstream * field)
                add(2, k, upstream * skip)

    sum_start(BACK_C, over_rows(3, residual_back))
    product_grad(lambda span: s.residual[inner, inner, :, span].reshape(points, LANES), c, at.second)
    jobs[0].scatter()
    s.square_t[...] = s.output_kernel[...].T
    shift_c, gain_c, gain_s = sum_finish(BACK_C)
    set_back(C_, shift_c, gain_c, inv_out, OUTPUT_G)
    set_back(S_, shift_c, gain_s, inv_out, SHORT_G)

    s.gathered[...] = jnp.zeros((ca, c), F32)

    def branch_back(r, add, add_image):
        masks, sources = masks_out(r), strided(r, 0, 0)
        for k in range(halves):
            skips = bypass(sources, k)
            for j in range(r_out):
                upstream, field = s.field[spot(r, j), lanes(k)], s.branch[spot(r, j), lanes(k)].astype(F32)
                s.cot[r, j, :, lanes(k)] = back(C_, upstream, field, masks[j], k)
                s.skip[j * n : (j + 1) * n, lanes(k)] = back(S_, upstream, part(skips, j), masks[j], k)
        s.gathered[...] += tm(sources, s.skip[...])
        s.upstream[rows(r), 0:ci] = mm(s.skip[...], s.start_rows[0:c, :])
        excited_back(r, add, add_image, B_, s.middle, 0)

    *sums_b, dscaling_sums = over(2, 1, branch_back)
    jobs[0].settle()
    excite_backward_start(3, 0, one, dscaling_sums)
    sum_start(BACK_B, sums_b)
    s.stage[at.shortcut : at.shortcut + ci, :] = s.gathered[0:ci, :].astype(BF16)
    product_grad(lambda span: s.excited_one[:, span], c, at.output)
    jobs[0].exchange()
    gates_wait(0, 3)
    excite_backward(3, one, 0)
    s.stage[at.biases : at.biases + 16, :] = s.biases[...].astype(BF16)
    jobs[0].gather()
    jobs[1].swap()
    set_back(B_, *finish_gate(BACK_B, 0), inv_out, GROUP_G)

    def put_middle(r, j, k, dz):
        s.frame[r, j, :, lanes(k)] = dz

    gate_back(B_, 0, 3, s.middle, put_middle)
    corners = corner_copies(s.frame)
    for copy in corners:
        copy.start()

    def all_one(ky, kx, q):
        return jnp.concatenate(
            [s.active[2 * i + ky, 2 * j + kx, :, quarter(q)] for i in range(r_out) for j in range(r_out)], axis=0
        )

    kernel_grad(lambda q: s.frame[outer, outer, :, quarter(q)].reshape(points, LANES), all_one, at.group)
    jobs[0].hand()
    jobs[1].scatter()
    jobs[2].swap()
    for copy in corners:
        copy.wait_recv()

    @pl.when(ha == d.ha - 1)
    def _():
        s.frame[r_out] = blank

    @pl.when(wa == d.wa - 1)
    def _():
        s.frame[:, r_out] = blank

    meets = {0: ((1, 0),), 1: ((0, 1), (2, 0))}
    parities = [(ph, pw) for ph in range(2) for pw in range(2)]

    def entry_sums(i, add):
        for ph, pw in parities:
            first, last = PARITY_SPANS[ph, pw]
            sources = strided(i, ph, pw)
            for k in range(halves):
                windows = [
                    s.frame[i + dr, pl.ds(dc, r_out), :, lanes(k)].reshape(block, half)
                    for _, dr in meets[ph]
                    for _, dc in meets[pw]
                ]
                window = windows[0] if len(windows) == 1 else jnp.concatenate(windows, axis=1)
                dactive = mm(window, s.taps[k, first * half : last * half, :])
                fields = mm(sources, s.entry_rows[:, lanes(k)])
                for j in range(r_out):
                    field = part(fields, j)
                    _, slope = silu_and_slope(field * keep(A_, 2, k))
                    mask = mask_at(row0 + 2 * i + ph, col0 + 2 * j + pw, half, 0.5)
                    upstream = part(dactive, j) * mask * slope
                    s.active[2 * i + ph + 1, 2 * j + pw + 1, :, lanes(k)] = upstream.astype(BF16)
                    add(0, k, upstream)
                    add(1, k, upstream * field)

    sums_e = over_rows(2, entry_sums)
    jobs[1].settle()
    sum_start(BACK_A, sums_e)
    jobs[1].exchange()
    jobs[2].scatter()
    s.gathered[...] = jnp.zeros((ca, c), F32)

    def meet(h):
        upstream = s.active[h + 1, pl.ds(1, h_in)].reshape(h_in * n, c)
        s.gathered[...] += tm(s.x[h].reshape(h_in * n, ca), upstream)

    each_row(meet, h_in)
    set_back(A_, *sum_finish(BACK_A), inv_in, ENTRY_G, raised)

    kernel_rows = s.entry_kernel[...].astype(F32)
    folded = jnp.concatenate([kernel_rows * keep(A_, 6), below([keep(A_, 7)])], axis=0)
    s.stage[at.entry : at.entry + ci, :] = (
        s.gathered[0:ci, :] * keep(A_, 5) + exact(mm, s.gram[0:ci, :], folded)
    ).astype(BF16)
    jobs[3].scatter()
    s.start_rows[0:c, :] = (kernel_rows * keep(A_, 5)).T.astype(BF16)
    high, low = in_parts(fine(mt, folded, s.entry_kernel[...]), 2)
    s.start_rows[c : c + ca, :] = high
    s.start_rows[c + ca : c + 2 * ca, :] = low
    jobs[1].gather()
    jobs[2].exchange()

    def store_row(h):
        return pltpu.make_async_copy(s.raw.at[h % depth], s.images_grad.at[h], s.load_sems.at[h % depth])

    def start_back(i):
        for ph in range(2):
            h = 2 * i + ph

            @pl.when(h >= depth)
            def _(h=h):
                store_row(h - depth).wait()

            for q in range(2):
                span = pl.ds(r_out * q, r_out)
                upstream = s.active[h + 1, pl.ds(1 + r_out * q, r_out)].reshape(block, c)
                x = s.x[h, span].reshape(block, ca)
                dstart = mm(jnp.concatenate([upstream, x, x], axis=1), s.start_rows[...])
                for j in range(r_out):
                    w = r_out * q + j
                    value = part(dstart, j)
                    if ph == 0 and w % 2 == 0:
                        value = value + s.upstream[spot(i, w // 2), 0:ci]
                    s.raw[h % depth, w] = value.astype(BF16)
            store_row(h).start()

    each_row(start_back, 2)
    jobs[3].exchange()
    jobs[1].hand()
    jobs[2].gather()
    each_row(start_back, r_out, 2)
    jobs[3].gather()
    jobs[2].hand()
    jobs[3].hand()


    for copy in rims + ring + ring_back + corners:
        copy.wait_send()
    for k in range(len(VECTORS)):
        sum_wait(k, 0)
        sum_wait_across(k, 2)
    for j in range(4):
        tiles_wait(j, 0)
    for which in range(2):
        gates_wait(which, 2)
        img_wait(which, 0)
    for h in range(h_in - depth, h_in):
        store_row(h).wait()
    for job in jobs:
        job.finish()


def run(d, operands):
    n, c, ci, r = d.images, d.channels, d.inputs, d.rows
    points, h_in, group = r * r * n, 2 * r, n // d.ha
    plane = d.ha * d.wa
    half = min(256, c)
    vm = functools.partial(pl.BlockSpec, memory_space=pltpu.VMEM)
    anywhere = functools.partial(pl.BlockSpec, memory_space=pl.ANY)
    smem = functools.partial(pl.BlockSpec, memory_space=pltpu.SMEM)
    inputs = dict(
        images=anywhere(), cotangent=anywhere(), classes=vm(), image_counts=smem(),
        **{name: anywhere() for name, _ in d.vectors},
        entry_kernel=vm(), shortcut_kernel=vm(), **{name + SENT: anywhere() for name in d.weights},
    )
    outputs = dict(
        activations=(jax.ShapeDtypeStruct((r, r, n, c), BF16), anywhere()),
        images_grad=(jax.ShapeDtypeStruct((h_in, h_in, n, ci), BF16), anywhere()),
        stage=(jax.ShapeDtypeStruct((d.grad_lines, c), BF16), vm()),
        vectors=(jax.ShapeDtypeStruct((16, c), F32), vm()),
    )
    dma = pltpu.SemaphoreType.DMA
    narrow = -(-2 * (c // LANES) // 8) * 8
    last = d.jobs[3][1] // d.ha
    sums, lines = len(VECTORS), d.grad_lines // (2 * d.ha) + last // 2
    scratch = dict(
        x=pltpu.VMEM((h_in, h_in, n, d.augmented), BF16),
        raw=pltpu.VMEM((2, h_in, n, ci), BF16),
        rim=pltpu.VMEM((2, h_in, n, ci), BF16),
        rim_corner=pltpu.VMEM((1, n, ci), BF16),
        rim_rows=pltpu.VMEM((r, n, d.augmented), BF16),
        active=pltpu.VMEM((h_in + 1, h_in + 1, n, c), BF16),
        cot=pltpu.VMEM((r, r, n, c), BF16),
        middle=pltpu.VMEM((points, c), BF16),
        branch=pltpu.VMEM((points, c), BF16),
        second=pltpu.VMEM((points, c), BF16),
        excited_one=pltpu.VMEM((points, c), BF16),
        residual=pltpu.VMEM((r + 2, r + 2, n, c), BF16),
        frame=pltpu.VMEM((r + 2, r + 2, n, c), BF16),
        spatial=pltpu.VMEM((points, c), BF16),
        excited_two=pltpu.VMEM((max(points, d.grad_lines - d.jobs[2][0]), c), BF16),
        field=pltpu.VMEM((points, c), F32),
        upstream=pltpu.VMEM((points, c), F32),
        dframe=pltpu.VMEM((r + 2, r + 2, n, c), BF16),
        skip=pltpu.VMEM((r * n, c), BF16),
        turned=pltpu.VMEM((c // LANES, LANES, points), BF16),
        taps=pltpu.VMEM((c // half, 9 * half, half), BF16),
        entry_rows=pltpu.VMEM((d.augmented, c), BF16),
        short_rows=pltpu.VMEM((d.augmented, c), BF16),
        start_rows=pltpu.VMEM((c + 2 * d.augmented, ci), BF16),
        gram=pltpu.VMEM((d.augmented, d.augmented), F32),
        square_t=pltpu.VMEM((c, c), BF16),
        gathered=pltpu.VMEM((d.augmented, c), F32),
        biases=pltpu.VMEM((16, c), F32),
        vec=pltpu.VMEM((24, c), F32),
        lim=pltpu.VMEM((n, LANES), jnp.int32),
        invpix=pltpu.VMEM((d.ha, group, LANES), F32),
        keep=pltpu.VMEM((56, c), F32),
        slots=pltpu.VMEM((sums, plane, narrow, LANES), F32),
        across=pltpu.VMEM((sums, d.img, narrow, LANES), F32),
        slots_wide=pltpu.VMEM((2, plane, 2 * narrow, LANES), F32),
        across_wide=pltpu.VMEM((2, d.img, 2 * narrow, LANES), F32),
        reduced=pltpu.VMEM((16, LANES), F32),
        tile_slots=pltpu.VMEM((4, plane, n, LANES), BF16),
        dlogit=pltpu.VMEM((n, c), F32),
        gate_src=pltpu.VMEM((d.ha, 2, group, c), BF16),
        gate_slots=pltpu.VMEM((plane, 2, group, c), BF16),
        shared=pltpu.VMEM((4, d.ha, group, c), F32),
        gates=pltpu.VMEM((2, d.ha, 2, group, c), F32),
        group_x=pltpu.VMEM((2, d.img, narrow, LANES), F32),
        pooled_one=pltpu.VMEM((n, c), F32),
        before_one=pltpu.VMEM((n, d.hidden_one), F32),
        pooled_two=pltpu.VMEM((n, c), F32),
        before_two=pltpu.VMEM((n, d.hidden_two), F32),
        swaps=pltpu.VMEM((d.grad_lines // 2, c), BF16),
        scattered=pltpu.VMEM((plane, lines, LANES), BF16),
        crossed=pltpu.VMEM((d.img // 2, lines, LANES), BF16),
        crossed_all=pltpu.VMEM((d.img, last, LANES), BF16),
        summed=pltpu.VMEM((lines, LANES), BF16),
        **{name: pltpu.VMEM(value.shape, BF16) for name, value in d.weights.items()},
        weight_sems=dma((len(d.weights),)),
        load_sems=dma((2,)),
        vec_sems=dma((len(d.vectors),)),
        cot_sem=dma((2,)),
        sum_sems=dma((sums, 4)),
        tile_sems=dma((4, 2)),
        gate_sems=dma((2, 4)),
        group_sems=dma((2, 2)),
        ring_send=dma((2, 8)),
        ring_recv=dma((2, 8)),
        rim_send=dma((3,)),
        rim_recv=dma((3,)),
        corner_send=dma((3,)),
        corner_recv=dma((3,)),
        grad_sems=dma((len(d.jobs), 10)),
    )
    d.names = [*inputs, *outputs, *scratch]
    return pl.pallas_call(
        functools.partial(kernel, d),
        out_shape=[shape for shape, _ in outputs.values()],
        in_specs=list(inputs.values()),
        out_specs=[spec for _, spec in outputs.values()],
        scratch_shapes=list(scratch.values()),
        compiler_params=pltpu.CompilerParams(
            collective_id=0, has_side_effects=True, vmem_limit_bytes=d.vmem, fuse_transposed_lhs_in_matmul=True
        ),
        name="blocks",
    )(*[operands[name] for name in inputs])


def widen(d, activations, images_grad, total, sums):
    names = [name for name, (_, size) in d.grad_rows.items() if size != 16]
    first_bias = [first for first, size in d.grad_rows.values() if size == 16][0]
    c, nch = d.channels, d.channels // LANES
    vectors = sums.shape[0]
    bias_sizes = (c, LANES, c, LANES)

    def shape_of(name):
        return (c, d.hidden_two) if name == d.chunked else (d.grad_rows[name][1], c)

    def widen_kernel(activations_in, images_in, total_sent, sums_in, *refs):
        outs, (total, *wide), (large_a, large_b, biases, sems, vec_sems, grad_sems) = (
            refs[: -len(names) - 7], refs[-len(names) - 7 : -6], refs[-6:]
        )
        activations_out, images_out, *rest = outs
        grads, lines = rest[: len(names)], rest[len(names) :]
        arriving = [
            pltpu.make_async_copy(images_in, large_a, sems.at[0]),
            pltpu.make_async_copy(activations_in, large_b, sems.at[1]),
        ]
        leaving = [
            pltpu.make_async_copy(large_a, images_out, sems.at[2]),
            pltpu.make_async_copy(large_b, activations_out, sems.at[3]),
        ]
        total_copy = pltpu.make_async_copy(total_sent, total, sems.at[4])
        total_copy.start()
        for copy in arriving:
            copy.start()
        total_copy.wait()
        biases[...] = total[first_bias : first_bias + 16, :].astype(F32)
        sources = [sums_in.at[i] for i in range(vectors)]
        sources += [biases.at[i, pl.ds(0, size)] for i, size in enumerate(bias_sizes)]
        small = [
            pltpu.make_async_copy(source, line, vec_sems.at[i])
            for i, (source, line) in enumerate(zip(sources, lines, strict=True))
        ]
        for copy in small:
            copy.start()
        grad_copies = []
        for i, (name, held, out) in enumerate(zip(names, wide, grads, strict=True)):
            first, size = d.grad_rows[name]
            if name == d.chunked:
                for q in range(nch):
                    chunk = total[first : first + size, q * LANES : (q + 1) * LANES]
                    held[q * LANES : (q + 1) * LANES, :] = chunk.astype(F32)
            else:
                held[...] = total[first : first + size, :].astype(F32)
            grad_copies.append(pltpu.make_async_copy(held, out, grad_sems.at[i]))
            grad_copies[-1].start()
            if i == 1:
                for into, onward in zip(arriving, leaving, strict=True):
                    into.wait()
                    onward.start()
        for copy in small + leaving + grad_copies:
            copy.wait()

    anywhere = pl.BlockSpec(memory_space=pl.ANY)
    inside = pl.BlockSpec(memory_space=pltpu.VMEM)
    line_sizes = (c,) * vectors + bias_sizes
    out = pl.pallas_call(
        widen_kernel,
        out_shape=[
            jax.ShapeDtypeStruct(activations.shape, BF16), jax.ShapeDtypeStruct(images_grad.shape, BF16),
            *[jax.ShapeDtypeStruct(shape_of(name), F32) for name in names],
            *[jax.ShapeDtypeStruct((size,), F32) for size in line_sizes],
        ],
        in_specs=[anywhere, anywhere, anywhere, inside],
        out_specs=[anywhere] * (2 + len(names) + len(line_sizes)),
        scratch_shapes=[
            pltpu.VMEM(total.shape, BF16), *[pltpu.VMEM(shape_of(name), F32) for name in names],
            pltpu.VMEM(images_grad.shape, BF16), pltpu.VMEM(activations.shape, BF16), pltpu.VMEM((16, c), F32),
            pltpu.SemaphoreType.DMA((5,)), pltpu.SemaphoreType.DMA((len(line_sizes),)),
            pltpu.SemaphoreType.DMA((len(names),)),
        ],
        compiler_params=pltpu.CompilerParams(vmem_limit_bytes=d.vmem),
        name="widen",
    )(activations, images_grad, total, sums)
    grads, lines = out[2 : 2 + len(names)], out[2 + len(names) :]
    return out[0], out[1], types.SimpleNamespace(**dict(zip(names, grads, strict=True))), lines


def body(
    images, classes, image_counts, entry_kernel, entry_gain, entry_shift, group_kernel, group_gain, group_shift,
    squeeze_weight, squeeze_bias, excite_weight, excite_bias, output_kernel, output_gain, output_shift,
    shortcut_kernel, shortcut_gain, shortcut_shift, second_kernel, second_gain, second_shift, spatial_kernel,
    spatial_gain, spatial_shift, reduce_weight, reduce_bias, expand_weight, expand_bias, final_kernel, final_gain,
    final_shift, cotangent,
):
    vectors = dict(
        entry_gain=entry_gain, entry_shift=entry_shift, group_gain=group_gain, group_shift=group_shift,
        output_gain=output_gain, output_shift=output_shift, shortcut_gain=shortcut_gain,
        shortcut_shift=shortcut_shift, second_gain=second_gain, second_shift=second_shift,
        spatial_gain=spatial_gain, spatial_shift=spatial_shift, final_gain=final_gain, final_shift=final_shift,
        excite_bias=excite_bias, expand_bias=expand_bias,
        squeeze_bias=jnp.pad(squeeze_bias, (0, -squeeze_bias.shape[0] % LANES)), reduce_bias=reduce_bias,
    )
    d = types.SimpleNamespace(
        ha=lax.axis_size("ha"), wa=lax.axis_size("wa"), img=lax.axis_size("img"),
        images=images.shape[0], rows=images.shape[1] // 2, inputs=images.shape[3],
        channels=entry_kernel.shape[1], width=group_kernel.shape[2],
        hidden_one=squeeze_weight.shape[1], hidden_two=reduce_weight.shape[1], vmem=64 * 1024 * 1024 - 65536,
        vectors=[(name, v.shape[0]) for name, v in vectors.items()],
    )
    n, c = d.images, d.channels
    d.grad_rows, d.jobs, d.grad_lines = grad_rows(c, d.inputs, d.hidden_one, d.hidden_two, d.width)
    d.augmented = -(-(d.inputs + 3) // LANES) * LANES
    d.chunked = list(d.grad_rows)[1]
    d.weights = dict(
        group_kernel=group_kernel.reshape(9, d.width, c), squeeze=squeeze_weight.T, excite=excite_weight,
        output_kernel=output_kernel, second_kernel=second_kernel,
        spatial_kernel=spatial_kernel.reshape(9, d.width, c), reduce=reduce_weight, expand=expand_weight,
        final_kernel=final_kernel,
    )
    operands = dict(
        **vectors,
        **{name + SENT: value for name, value in d.weights.items()},
        images=images.transpose(1, 2, 0, 3),
        cotangent=cotangent.transpose(1, 2, 0, 3),
        classes=classes.reshape(d.img, n),
        image_counts=image_counts,
        entry_kernel=entry_kernel,
        shortcut_kernel=shortcut_kernel,
    )
    activations, images_grad, total, sums = run(d, operands)
    activations, images_grad, g, lines = widen(d, activations, images_grad, total, sums)
    biases = lines[-4:]

    def taps_of(v):
        return v.reshape(3, 3, d.width, c)

    def pair(i):
        return lines[i], lines[i + 1]

    return (
        activations.transpose(2, 0, 1, 3),
        images_grad.transpose(2, 0, 1, 3),
        g.entry, *pair(ENTRY_G),
        taps_of(g.group), *pair(GROUP_G),
        g.squeeze.T, biases[1][: d.hidden_one], g.excite, biases[0],
        g.output, *pair(OUTPUT_G),
        g.shortcut, *pair(SHORT_G),
        g.second, *pair(SECOND_G),
        taps_of(g.spatial), *pair(SPATIAL_G),
        g.reduce, biases[3][: d.hidden_two], g.expand, biases[2],
        g.final, *pair(FINAL_G),
    )


def solution(mesh):
    spread = P("img", "ha", "wa", None)
    return jax.shard_map(
        body,
        mesh=mesh,
        in_specs=(spread, *[P()] * 31, spread),
        out_specs=(spread, spread, *[P()] * 29),
        check_vma=False,
    )
```
